32 devices in a mesh: seg: 16 (over z, y, core), item: 2 (over x).
Axes of the slice: x: 2, y: 2, z: 4, core: 2. Of those that a mesh axis runs over, the one named last changes fastest.
Arguments:
- text: bfloat16 [8, 16, 64, 768], P('item', 'seg'), may hold values from -6 to 6
- cotangent: bfloat16 [8, 16, 84, 768], P('item', 'seg'), may hold values from -6 to 6
- unroll: int32 [8], P('item'), may hold values from 1 to 16, as said below
- memory: bfloat16 [10, 768], replicated, may hold values from -6 to 6
- qkv_weight: bfloat16 [768, 2304], P('seg'), may hold values from -0.21875 to 0.21875
- qv_bias: bfloat16 [1536], P('seg'), may hold values from -3 to 3
- out_weight: bfloat16 [768, 768], P('seg'), may hold values from -2 to 2
- out_bias: bfloat16 [768], P('seg'), may hold values from -3 to 3
- norm1_gain: bfloat16 [768], P('seg'), may hold values from 0.099609375 to 1.8984375
- norm1_bias: bfloat16 [768], P('seg'), may hold values from -3 to 3
- up_weight: bfloat16 [768, 3072], P('seg'), may hold values from -0.21875 to 0.21875
- up_bias: bfloat16 [3072], P('seg'), may hold values from -3 to 3
- down_weight: bfloat16 [3072, 768], P('seg'), may hold values from -0.109375 to 0.109375
- down_bias: bfloat16 [768], P('seg'), may hold values from -3 to 3
- norm2_gain: bfloat16 [768], P('seg'), may hold values from 0.099609375 to 1.8984375
- norm2_bias: bfloat16 [768], P('seg'), may hold values from -3 to 3
- deep_qkv_weight: bfloat16 [768, 2304], P('seg'), may hold values from -0.21875 to 0.21875
- deep_qv_bias: bfloat16 [1536], P('seg'), may hold values from -3 to 3
- deep_out_weight: bfloat16 [768, 768], P('seg'), may hold values from -2 to 2
- deep_out_bias: bfloat16 [768], P('seg'), may hold values from -3 to 3
- deep_norm1_gain: bfloat16 [768], P('seg'), may hold values from 0.099609375 to 1.8984375
- deep_norm1_bias: bfloat16 [768], P('seg'), may hold values from -3 to 3
- deep_up_weight: bfloat16 [768, 3072], P('seg'), may hold values from -0.21875 to 0.21875
- deep_up_bias: bfloat16 [3072], P('seg'), may hold values from -3 to 3
- deep_down_weight: bfloat16 [3072, 768], P('seg'), may hold values from -0.109375 to 0.109375
- deep_down_bias: bfloat16 [768], P('seg'), may hold values from -3 to 3
- deep_norm2_gain: bfloat16 [768], P('seg'), may hold values from 0.099609375 to 1.8984375
- deep_norm2_bias: bfloat16 [768], P('seg'), may hold values from -3 to 3
Outputs:
- layer_out: bfloat16 [8, 16, 84, 768], P('item', 'seg')
- text_grad: float32 [8, 16, 64, 768], P('item', 'seg')
- memory_grad: float32 [10, 768], P(None, 'seg')
- qkv_weight_grad: float32 [768, 2304], P('seg')
- qv_bias_grad: float32 [1536], P('seg')
- out_weight_grad: float32 [768, 768], P('seg')
- out_bias_grad: float32 [768], P('seg')
- norm1_gain_grad: float32 [768], P('seg')
- norm1_bias_grad: float32 [768], P('seg')
- up_weight_grad: float32 [768, 3072], P('seg')
- up_bias_grad: float32 [3072], P('seg')
- down_weight_grad: float32 [3072, 768], P('seg')
- down_bias_grad: float32 [768], P('seg')
- norm2_gain_grad: float32 [768], P('seg')
- norm2_bias_grad: float32 [768], P('seg')
- deep_qkv_weight_grad: float32 [768, 2304], P('seg')
- deep_qv_bias_grad: float32 [1536], P('seg')
- deep_out_weight_grad: float32 [768, 768], P('seg')
- deep_out_bias_grad: float32 [768], P('seg')
- deep_norm1_gain_grad: float32 [768], P('seg')
- deep_norm1_bias_grad: float32 [768], P('seg')
- deep_up_weight_grad: float32 [768, 3072], P('seg')
- deep_up_bias_grad: float32 [3072], P('seg')
- deep_down_weight_grad: float32 [3072, 768], P('seg')
- deep_down_bias_grad: float32 [768], P('seg')
- deep_norm2_gain_grad: float32 [768], P('seg')
- deep_norm2_bias_grad: float32 [768], P('seg')
The draws below stay inside these ranges and needn't reach their ends.
Inputs may be any that keep to these rules, and one draw needn't show every extreme that they name: Among the items of each aligned group of 4 items (one index of item) at least one has unroll 16.
All inputs are finite; a program needn't handle non-finite values.
Results may differ from the reference program's by a relative error of at most 0.029.
Values may be sent and summed in bfloat16 or wider, within the bound.
No kernel may reach another device: no remote copies, remote signals or barrier semaphores. Data moves between devices by JAX's collectives and lax.ppermute only.
A program may use at most 256 MiB of HBM per device.

```python
import jax
import jax.numpy as jnp
from jax import lax

D = 768
HEADS = 12
HEAD_DIM = 64
FF = 3072
MEM = 10
TEXT = 64
ROWS = 84
SEGS = 16
MICRO = 4
ITEMS = 8


def draw_unroll(key, part):
    key = jax.random.fold_in(key, 7)
    first, second = jax.random.split(key)
    groups = ITEMS // MICRO
    counts = jax.random.randint(first, (groups, MICRO), 1, SEGS + 1)
    chosen = jax.random.randint(second, (groups, 1), 0, MICRO)
    slots = jnp.arange(MICRO, dtype=jnp.int32)[None, :]
    counts = jnp.where(slots == chosen, SEGS, counts)
    return counts.reshape(ITEMS).astype(jnp.int32)


def level_of(key, shape, shards, low, largest):
    level = 1.0
    for dim, parts in shards:
        steps = jax.random.uniform(jax.random.fold_in(jax.random.fold_in(key, 6), dim), (parts,), jnp.float32, low / len(shards), largest / len(shards))
        level = level * jnp.repeat(jnp.exp(steps), shape[dim] // parts).reshape((-1,) + (1,) * (len(shape) - 1 - dim))
    return level


def noise(key, shape, scale, most, shards=(), kind=jnp.bfloat16):
    array = scale * jax.random.normal(key, shape, jnp.float32)
    if shards:
        array = array * level_of(key, shape, shards, -0.22, 0.18)
    return jnp.clip(array, -most, most).astype(kind)


def setup_inputs(seed: int = 0) -> dict:
    seeds = jax.random.split(jax.random.key(seed), 29)
    return {
        "text": noise(seeds[0], (ITEMS, SEGS, TEXT, D), 1.0, 6.0, ((0, 2), (1, 16))),
        "cotangent": noise(seeds[1], (ITEMS, SEGS, ROWS, D), 1.0, 6.0, ((0, 2), (1, 16))),
        "unroll": draw_unroll(jax.random.fold_in(seeds[28], 71), 0),
        "memory": noise(seeds[3], (MEM, D), 1.0, 6.0),
        "qkv_weight": noise(seeds[4], (D, 3 * D), D ** -0.5, 0.21875, ((0, 16),)),
        "qv_bias": noise(seeds[5], (2 * D,), 0.5, 3.0, ((0, 16),)),
        "out_weight": noise(seeds[6], (D, D), (max(D // ROWS, 1)) ** -0.5, 2.0, ((0, 16),)),
        "out_bias": noise(seeds[7], (D,), 0.5, 3.0, ((0, 16),)),
        "norm1_gain": jnp.clip(1.0 + 0.18 * jax.random.normal(seeds[8], (D,), jnp.float32), 0.099609375, 1.8984375).astype(jnp.bfloat16),
        "norm1_bias": noise(seeds[9], (D,), 0.5, 3.0, ((0, 16),)),
        "up_weight": noise(seeds[10], (D, FF), D ** -0.5, 0.21875, ((0, 16),)),
        "up_bias": noise(seeds[11], (FF,), 0.5, 3.0, ((0, 16),)),
        "down_weight": noise(seeds[12], (FF, D), FF ** -0.5, 0.109375, ((0, 16),)),
        "down_bias": noise(seeds[13], (D,), 0.5, 3.0, ((0, 16),)),
        "norm2_gain": jnp.clip(1.0 + 0.18 * jax.random.normal(seeds[14], (D,), jnp.float32), 0.099609375, 1.8984375).astype(jnp.bfloat16),
        "norm2_bias": noise(seeds[15], (D,), 0.5, 3.0, ((0, 16),)),
        "deep_qkv_weight": noise(seeds[16], (D, 3 * D), D ** -0.5, 0.21875, ((0, 16),)),
        "deep_qv_bias": noise(seeds[17], (2 * D,), 0.5, 3.0, ((0, 16),)),
        "deep_out_weight": noise(seeds[18], (D, D), (max(D // ROWS, 1)) ** -0.5, 2.0, ((0, 16),)),
        "deep_out_bias": noise(seeds[19], (D,), 0.5, 3.0, ((0, 16),)),
        "deep_norm1_gain": jnp.clip(1.0 + 0.18 * jax.random.normal(seeds[20], (D,), jnp.float32), 0.099609375, 1.8984375).astype(jnp.bfloat16),
        "deep_norm1_bias": noise(seeds[21], (D,), 0.5, 3.0, ((0, 16),)),
        "deep_up_weight": noise(seeds[22], (D, FF), D ** -0.5, 0.21875, ((0, 16),)),
        "deep_up_bias": noise(seeds[23], (FF,), 0.5, 3.0, ((0, 16),)),
        "deep_down_weight": noise(seeds[24], (FF, D), FF ** -0.5, 0.109375, ((0, 16),)),
        "deep_down_bias": noise(seeds[25], (D,), 0.5, 3.0, ((0, 16),)),
        "deep_norm2_gain": jnp.clip(1.0 + 0.18 * jax.random.normal(seeds[26], (D,), jnp.float32), 0.099609375, 1.8984375).astype(jnp.bfloat16),
        "deep_norm2_bias": noise(seeds[27], (D,), 0.5, 3.0, ((0, 16),)),
    }


epsilon = 1e-05
highest = lax.Precision.HIGHEST

@jax.custom_vjp
def low(v):
    return lax.optimization_barrier(v.astype(jnp.bfloat16)).astype(jnp.float32)

@jax.custom_vjp
def low_back(v):
    return v

def low_keep(v):
    return (low(v), None)

def low_pass(kept, grad):
    return (grad,)

def back_keep(v):
    return (v, None)

def back_low(kept, grad):
    return (low(grad),)
low.defvjp(low_keep, low_pass)
low_back.defvjp(back_keep, back_low)

def norm_rows(total, gain, shift):
    centre = total - lax.optimization_barrier(jnp.mean(total, -1, keepdims=True))
    spread = lax.optimization_barrier(jnp.mean(centre * centre, -1, keepdims=True))
    return centre * lax.rsqrt(spread + epsilon) * gain + shift

def project(left, right):
    return jnp.einsum('bre,ef->brf', left, right, precision=highest)

def layer(inputs, params):
    qkv_weight, qv_bias, out_weight, out_bias, norm1_gain, norm1_bias, up_weight, up_bias, down_weight, down_bias, norm2_gain, norm2_bias = params
    batch, rows, width = inputs.shape
    bias_full = jnp.concatenate([qv_bias[:width], jnp.zeros((width,), jnp.float32), qv_bias[width:]])
    qkv = low_back(low(project(low(inputs), qkv_weight) + bias_full))
    heads = qkv.reshape(batch, rows, 3, HEADS, HEAD_DIM)
    query = heads[:, :, 0]
    keys = heads[:, :, 1]
    values = heads[:, :, 2]
    scores = low_back(jnp.einsum('bqhe,bkhe->bhqk', query, keys, precision=highest) * HEAD_DIM ** (-0.5))
    probs = jax.nn.softmax(scores, axis=-1)
    context = jnp.einsum('bhqk,bkhe->bqhe', low(probs), values, precision=highest).reshape(batch, rows, width)
    context = low_back(low(context))
    first = inputs + low_back(project(context, out_weight) + out_bias)
    hidden = norm_rows(first, norm1_gain, norm1_bias)
    upper = low_back(project(low(hidden), up_weight) + up_bias)
    activated = low(jax.nn.gelu(upper, approximate=False))
    second = hidden + low_back(project(activated, down_weight) + down_bias)
    return norm_rows(second, norm2_gain, norm2_bias)

def forward(text, memory, params_one, params_two, unroll):
    items = text.shape[0]
    placeholders = jnp.broadcast_to(memory, (items, MEM, D))

    def step(carry, inputs):
        index, text_seg = inputs
        fresh = jnp.logical_or(index == 0, unroll == index)
        read = jnp.where(fresh[:, None, None], placeholders, low_back(low(carry)))
        middle = layer(jnp.concatenate([read, text_seg, placeholders], axis=1), params_one)
        result = layer(middle, params_two)
        return (result[:, ROWS - MEM:], result)
    start = jnp.zeros((items, MEM, D), jnp.float32)
    segments = jnp.arange(SEGS, dtype=jnp.int32)
    _, results = lax.scan(jax.checkpoint(step), start, (segments, jnp.swapaxes(text, 0, 1)))
    return jnp.swapaxes(results, 0, 1)

def reference(text, cotangent, unroll, memory, qkv_weight, qv_bias, out_weight, out_bias, norm1_gain, norm1_bias, up_weight, up_bias, down_weight, down_bias, norm2_gain, norm2_bias, deep_qkv_weight, deep_qv_bias, deep_out_weight, deep_out_bias, deep_norm1_gain, deep_norm1_bias, deep_up_weight, deep_up_bias, deep_down_weight, deep_down_bias, deep_norm2_gain, deep_norm2_bias):
    params = tuple((item.astype(jnp.float32) for item in (qkv_weight, qv_bias, out_weight, out_bias, norm1_gain, norm1_bias, up_weight, up_bias, down_weight, down_bias, norm2_gain, norm2_bias, deep_qkv_weight, deep_qv_bias, deep_out_weight, deep_out_bias, deep_norm1_gain, deep_norm1_bias, deep_up_weight, deep_up_bias, deep_down_weight, deep_down_bias, deep_norm2_gain, deep_norm2_bias)))

    def whole(text_in, memory_in, *weights):
        return forward(text_in, memory_in, weights[:12], weights[12:], unroll)
    result, pull = jax.vjp(whole, text.astype(jnp.float32), memory.astype(jnp.float32), *params)
    grads = pull(cotangent.astype(jnp.float32))
    return (result.astype(jnp.bfloat16), grads[0], grads[1], grads[2], grads[3], grads[4], grads[5], grads[6], grads[7], grads[8], grads[9], grads[10], grads[11], grads[12], grads[13], grads[14], grads[15], grads[16], grads[17], grads[18], grads[19], grads[20], grads[21], grads[22], grads[23], grads[24], grads[25])
```

```python
import jax
import jax.numpy as jnp
from jax import lax
from jax.experimental import pallas as pl
from jax.experimental.pallas import tpu as pltpu
from jax.sharding import PartitionSpec as P

HEAD_DIM = 64
EPSILON = 1e-05
F32 = jnp.float32
LOW = jnp.bfloat16
NN = (((1,), (0,)), ((), ()))
NT = (((1,), (1,)), ((), ()))
TN = (((0,), (0,)), ((), ()))

PAD = 16
BLOCKS = 12
B_QUERY, B_VALUE, B_OUT, GAIN1, SHIFT1, B_UP, B_DOWN, GAIN2, SHIFT2 = 0, 1, 2, 3, 4, 5, 9, 10, 11


def dot(left, right, dims=NN):
    return lax.dot_general(left, right, dims, preferred_element_type=F32)


def norm_rows(total, gain, shift):
    centre = total - jnp.mean(total, -1, keepdims=True)
    scale = lax.rsqrt(jnp.mean(centre * centre, -1, keepdims=True) + EPSILON)
    unit = centre * scale
    return unit, scale, unit * gain + shift


def norm_back(grad, unit, scale, gain):
    t = grad * gain
    return scale * (
        t - jnp.mean(t, -1, keepdims=True) - unit * jnp.mean(t * unit, -1, keepdims=True)
    )


def gelu_and_slope(upper):
    density = jnp.exp(upper * upper * -0.5) * 0.3989422804014327
    below = 0.5 * (1.0 + lax.erf(upper * 0.7071067811865476))
    return upper * below, below + upper * density


def fold(block):
    rows, width = block.shape
    return jnp.sum(block.reshape(rows // 8, 8, width), 0)


def two_heads(block, first):
    zero = jnp.zeros_like(block)
    return jnp.concatenate([jnp.where(first, block, zero), jnp.where(first, zero, block)], 0)


def load_weights(gathered, held, width, sem):
    shards = gathered.shape[0]
    part = width // shards

    def copies(shard):
        out = []
        for layer in range(2):
            src, dst = layer * BLOCKS * part, layer * BLOCKS * width
            for block in range(8):
                out.append((src + block * part, dst + block * width + shard * part, part))
            out.append((src + 8 * part, dst + 8 * width + shard * 4 * part, 4 * part))
        return [
            pltpu.make_async_copy(
                gathered.at[shard, pl.ds(a, n)], held.at[pl.ds(pl.multiple_of(b, 16), n)], sem
            )
            for a, b, n in out
        ]

    def start(shard, none):
        for copy in copies(shard):
            copy.start()
        return none

    def wait(shard, none):
        for copy in copies(shard):
            copy.wait()
        return none

    lax.fori_loop(0, shards, start, 0)
    lax.fori_loop(0, shards, wait, 0)


def forward_kernel(
    fresh_ref, text_ref, memory_ref, vector_ref, gathered_ref,
    low_ref, qkv_ref, probs_ref, context_ref, unit1_ref, hidden_ref, active_ref, slope_ref,
    unit2_ref, scale_ref, out_ref,
    held, carry, state, sem,
):
    step = pl.program_id(0)
    rows, width = state.shape
    texts = rows - 2 * PAD
    mem = 10

    @pl.when(step == 0)
    def _():
        load_weights(gathered_ref, held, width, sem)
        carry[...] = jnp.zeros_like(carry)

    column = lax.broadcasted_iota(jnp.int32, (2 * rows, rows), 1)
    unused = jnp.logical_or(
        column >= texts + PAD + mem,
        jnp.logical_and(column >= texts + mem, column < texts + PAD),
    )
    mask = jnp.where(unused, -1e30, 0.0).astype(F32)
    first_head = lax.broadcasted_iota(jnp.int32, (rows, 2 * HEAD_DIM), 1) < HEAD_DIM

    memory = memory_ref[...]
    state[:texts] = text_ref[0].astype(F32)
    state[texts : texts + PAD] = jnp.where(fresh_ref[step] > 0, memory, carry[...]).astype(F32)
    state[texts + PAD :] = memory.astype(F32)

    def layer(index, none):
        def weight(block):
            return held[pl.ds(pl.multiple_of((index * BLOCKS + block) * width, width), width), :]

        def vector(row):
            return vector_ref[index, row : row + 1, :]

        x = state[...]
        low = x.astype(LOW)
        low_ref[0, index] = low
        query = (dot(low, weight(0)) + vector(B_QUERY)).astype(LOW)
        keys = dot(low, weight(1)).astype(LOW)
        values = (dot(low, weight(2)) + vector(B_VALUE)).astype(LOW)
        qkv_ref[0, index, :, :width] = query
        qkv_ref[0, index, :, width : 2 * width] = keys
        qkv_ref[0, index, :, 2 * width :] = values
        for pair in range(width // (2 * HEAD_DIM)):
            cols = slice(2 * HEAD_DIM * pair, 2 * HEAD_DIM * (pair + 1))
            scores = dot(two_heads(query[:, cols], first_head), keys[:, cols], NT)
            scores = scores * HEAD_DIM ** (-0.5) + mask
            weights = jnp.exp(scores - jnp.max(scores, -1, keepdims=True))
            probs = (weights / jnp.sum(weights, -1, keepdims=True)).astype(LOW)
            probs_ref[0, index, pair] = probs
            both = dot(probs, values[:, cols])
            context_ref[0, index, :, cols] = jnp.where(
                first_head, both[:rows], both[rows:]
            ).astype(LOW)
        first = x + dot(context_ref[0, index], weight(3)) + vector(B_OUT)
        unit, scale, hidden = norm_rows(first, vector(GAIN1), vector(SHIFT1))
        unit1_ref[0, index] = unit.astype(LOW)
        scale_ref[0, index, 0] = jnp.broadcast_to(scale, (rows, 128))
        hidden_low = hidden.astype(LOW)
        hidden_ref[0, index] = hidden_low
        second = hidden + vector(B_DOWN)
        for block in range(4):
            cols = slice(block * width, (block + 1) * width)
            upper = dot(hidden_low, weight(4 + block)) + vector(B_UP + block)
            active, slope = gelu_and_slope(upper)
            active = active.astype(LOW)
            active_ref[0, index, :, cols] = active
            slope_ref[0, index, :, cols] = slope.astype(LOW)
            second = second + dot(active, weight(8 + block))
        unit, scale, final = norm_rows(second, vector(GAIN2), vector(SHIFT2))
        unit2_ref[0, index] = unit.astype(LOW)
        scale_ref[0, index, 1] = jnp.broadcast_to(scale, (rows, 128))
        state[...] = final
        return none

    lax.fori_loop(0, 2, layer, 0)
    final = state[...].astype(LOW)
    out_ref[0] = final
    carry[...] = final[texts + PAD :]


def backward_kernel(
    fresh_ref, cotangent_ref, vector_ref, qkv_ref, probs_ref, unit1_ref, slope_ref, unit2_ref,
    scale_ref, gathered_ref,
    grad_qkv_ref, grad_proj_ref, grad_upper_ref, grad_down_ref, text_ref, narrow_ref, wide_ref,
    memory_ref,
    held, carry, state, sem,
):
    turn = pl.program_id(0)
    step = pl.num_programs(0) - 1 - turn
    rows, width = state.shape
    texts = rows - 2 * PAD

    @pl.when(turn == 0)
    def _():
        load_weights(gathered_ref, held, width, sem)
        carry[...] = jnp.zeros_like(carry)
        narrow_ref[...] = jnp.zeros_like(narrow_ref)
        wide_ref[...] = jnp.zeros_like(wide_ref)
        memory_ref[...] = jnp.zeros_like(memory_ref)

    first_head = lax.broadcasted_iota(jnp.int32, (rows, 2 * HEAD_DIM), 1) < HEAD_DIM
    state[: texts + PAD] = cotangent_ref[0, : texts + PAD].astype(F32)
    state[texts + PAD :] = cotangent_ref[0, texts + PAD :].astype(F32) + carry[...].astype(F32)

    def layer(turned, none):
        index = 1 - turned

        def weight(block):
            return held[pl.ds(pl.multiple_of((index * BLOCKS + block) * width, width), width), :]

        def vector(row):
            return vector_ref[index, row : row + 1, :]

        grad = state[...]
        unit = unit2_ref[0, index].astype(F32)
        narrow_ref[index, 0] += fold(grad * unit)
        narrow_ref[index, 1] += fold(grad)
        grad_second = norm_back(grad, unit, scale_ref[0, index, 1, :, 0:1], vector(GAIN2))
        narrow_ref[index, 2] += fold(grad_second)
        grad_down = grad_second.astype(LOW)
        grad_hidden = grad_second
        for block in range(4):
            cols = slice(block * width, (block + 1) * width)
            grad_upper = dot(grad_down, weight(8 + block), NT) * slope_ref[0, index, :, cols].astype(F32)
            wide_ref[index, block] += fold(grad_upper)
            grad_upper = grad_upper.astype(LOW)
            grad_upper_ref[0, index, :, cols] = grad_upper
            grad_hidden = grad_hidden + dot(grad_upper, weight(4 + block), NT)
        grad_down_ref[0, index] = grad_down
        unit = unit1_ref[0, index].astype(F32)
        narrow_ref[index, 3] += fold(grad_hidden * unit)
        narrow_ref[index, 4] += fold(grad_hidden)
        grad_first = norm_back(grad_hidden, unit, scale_ref[0, index, 0, :, 0:1], vector(GAIN1))
        narrow_ref[index, 5] += fold(grad_first)
        grad_proj = grad_first.astype(LOW)
        grad_proj_ref[0, index] = grad_proj
        grad_context = dot(grad_proj, weight(3), NT).astype(LOW)
        for pair in range(width // (2 * HEAD_DIM)):
            cols = slice(2 * HEAD_DIM * pair, 2 * HEAD_DIM * (pair + 1))
            in_keys = slice(width + cols.start, width + cols.stop)
            in_values = slice(2 * width + cols.start, 2 * width + cols.stop)
            query = two_heads(qkv_ref[0, index, :, cols], first_head)
            keys = qkv_ref[0, index, :, in_keys]
            values = qkv_ref[0, index, :, in_values]
            context = two_heads(grad_context[:, cols], first_head)
            probs_low = probs_ref[0, index, pair]
            probs = probs_low.astype(F32)
            term = dot(context, values, NT) * probs
            grad_scores = term - probs * jnp.sum(term, -1, keepdims=True)
            grad_scores = (grad_scores * HEAD_DIM ** (-0.5)).astype(LOW)
            both = dot(grad_scores, keys)
            grad_query = jnp.where(first_head, both[:rows], both[rows:])
            grad_keys = dot(grad_scores, query, TN)
            grad_values = dot(probs_low, context, TN)
            narrow_ref[index, 6, :, cols] += fold(grad_query)
            narrow_ref[index, 7, :, cols] += fold(grad_values)
            grad_qkv_ref[0, index, :, cols] = grad_query.astype(LOW)
            grad_qkv_ref[0, index, :, in_keys] = grad_keys.astype(LOW)
            grad_qkv_ref[0, index, :, in_values] = grad_values.astype(LOW)
        grad_inputs = grad_first
        for block in range(3):
            cols = slice(block * width, (block + 1) * width)
            grad_inputs = grad_inputs + dot(grad_qkv_ref[0, index, :, cols], weight(block), NT)
        state[...] = grad_inputs
        return none

    lax.fori_loop(0, 2, layer, 0)
    text_ref[0] = state[:texts].astype(LOW)
    read = state[texts : texts + PAD]
    fresh = fresh_ref[step] > 0
    memory_ref[...] += state[texts + PAD :] + jnp.where(fresh, read, 0.0)
    carry[...] = jnp.where(fresh, 0.0, read).astype(LOW)


SMEM = pl.BlockSpec(memory_space=pltpu.SMEM)
VMEM = pl.BlockSpec(memory_space=pltpu.VMEM)
ANY = pl.BlockSpec(memory_space=pl.ANY)


def scratch(rows, width):
    return [
        pltpu.VMEM((2 * BLOCKS * width, width), LOW),
        pltpu.VMEM((PAD, width), LOW),
        pltpu.VMEM((rows, width), F32),
        pltpu.SemaphoreType.DMA,
    ]


def cost(rows, width, segments):
    return pl.CostEstimate(
        flops=2 * rows * 2 * BLOCKS * width * width * segments,
        bytes_accessed=2 * 2 * BLOCKS * width * width,
        transcendentals=0,
    )


def forward_chain(fresh, text, memory, vectors, gathered):
    segments, texts, width = text.shape
    rows = texts + 2 * PAD
    pairs = width // (2 * HEAD_DIM)

    def block(shape):
        return pl.BlockSpec((1,) + shape, lambda s: (s,) + (0,) * len(shape))

    outs = [
        ((2, rows, width), LOW),
        ((2, rows, 3 * width), LOW),
        ((2, pairs, 2 * rows, rows), LOW),
        ((2, rows, width), LOW),
        ((2, rows, width), LOW),
        ((2, rows, width), LOW),
        ((2, rows, 4 * width), LOW),
        ((2, rows, 4 * width), LOW),
        ((2, rows, width), LOW),
        ((2, 2, rows, 128), F32),
        ((rows, width), LOW),
    ]
    return pl.pallas_call(
        forward_kernel,
        grid=(segments,),
        in_specs=[SMEM, block((texts, width)), VMEM, VMEM, ANY],
        out_specs=[block(shape) for shape, _ in outs],
        out_shape=[jax.ShapeDtypeStruct((segments,) + shape, kind) for shape, kind in outs],
        scratch_shapes=scratch(rows, width),
        compiler_params=pltpu.CompilerParams(vmem_limit_bytes=62 << 20),
        cost_estimate=cost(rows, width, segments),
        name="forward_chain",
    )(fresh, text, memory, vectors, gathered)


def backward_chain(fresh, cotangent, vectors, qkv, probs, unit1, slope, unit2, scale, gathered):
    segments, rows, width = cotangent.shape
    texts = rows - 2 * PAD
    pairs = width // (2 * HEAD_DIM)

    def block(shape):
        return pl.BlockSpec((1,) + shape, lambda t: (segments - 1 - t,) + (0,) * len(shape))

    outs = [
        ((2, rows, 3 * width), LOW),
        ((2, rows, width), LOW),
        ((2, rows, 4 * width), LOW),
        ((2, rows, width), LOW),
        ((texts, width), LOW),
    ]
    return pl.pallas_call(
        backward_kernel,
        grid=(segments,),
        in_specs=[
            SMEM,
            block((rows, width)),
            VMEM,
            block((2, rows, 3 * width)),
            block((2, pairs, 2 * rows, rows)),
            block((2, rows, width)),
            block((2, rows, 4 * width)),
            block((2, rows, width)),
            block((2, 2, rows, 128)),
            ANY,
        ],
        out_specs=[block(shape) for shape, _ in outs] + [VMEM, VMEM, VMEM],
        out_shape=[jax.ShapeDtypeStruct((segments,) + shape, kind) for shape, kind in outs]
        + [
            jax.ShapeDtypeStruct((2, 8, 8, width), F32),
            jax.ShapeDtypeStruct((2, 4, 8, width), F32),
            jax.ShapeDtypeStruct((PAD, width), F32),
        ],
        scratch_shapes=scratch(rows, width),
        input_output_aliases={3: 0, 5: 1, 6: 2, 7: 3},
        compiler_params=pltpu.CompilerParams(vmem_limit_bytes=62 << 20),
        cost_estimate=cost(rows, width, segments),
        name="backward_chain",
    )(fresh, cotangent, vectors, qkv, probs, unit1, slope, unit2, scale, gathered)


def split_columns(shard, width):
    rows, columns = shard.shape
    return [shard[:, i : i + width] for i in range(0, columns, width)]


def body(text, cotangent, unroll, memory, *weights):
    micro, _, texts, width = text.shape
    mem = memory.shape[0]
    chain = lax.axis_size("seg")
    place = lax.axis_index("seg")
    stride = 2 if 2 * micro <= chain else 1
    start = (chain - stride * micro) // 2
    homes = [start + stride * i for i in range(micro)]
    layers = (weights[:12], weights[12:])

    vectors = jnp.concatenate([v for w in layers for v in w if v.ndim == 1])
    vectors = lax.all_gather(vectors, "seg").astype(F32)
    shards = []
    for w in layers:
        for matrix in (w[0], w[2], w[6], w[8]):
            shards += split_columns(matrix, width)
    gathered = lax.all_gather(jnp.concatenate(shards), "seg")
    part = width // chain
    if part % 16:
        together = 16 // (part & -part) if part & -part < 16 else 1
        gathered = regroup(gathered, together, part)
    rows_of = []
    at = 0
    for w in layers:
        for v in w:
            if v.ndim == 1:
                rows_of.append(vectors[:, at : at + v.shape[0]].reshape(-1, width))
                at += v.shape[0]
    half = len(rows_of) // 2
    table = jnp.stack([jnp.concatenate(rows_of[:half]), jnp.concatenate(rows_of[half:])])
    table = jnp.pad(table, ((0, 0), (0, 16 - table.shape[1]), (0, 0)))

    def to_home(blocks):
        empty = jnp.zeros(blocks.shape[1:], blocks.dtype)
        lanes = [blocks[homes.index(d)] if d in homes else empty for d in range(chain)]
        return lax.all_to_all(jnp.stack(lanes), "seg", 0, 0, tiled=True)

    def from_home(blocks):
        back = lax.all_to_all(blocks, "seg", 0, 0, tiled=True)
        return jnp.stack([back[d] for d in homes])

    def order(block):
        zero = jnp.zeros((block.shape[0], PAD - mem, width), block.dtype)
        return jnp.concatenate(
            [block[:, mem : mem + texts], block[:, :mem], zero, block[:, mem + texts :], zero], 1
        )

    def disorder(block):
        return jnp.concatenate(
            [
                block[:, texts : texts + mem],
                block[:, :texts],
                block[:, texts + PAD : texts + PAD + mem],
            ],
            1,
        )

    limit = unroll[jnp.clip((place - start) // stride, 0, micro - 1)]
    segments = jnp.arange(chain, dtype=jnp.int32)
    fresh = jnp.logical_or(segments == 0, segments == limit).astype(jnp.int32)
    memory_rows = jnp.pad(memory, ((0, PAD - mem), (0, 0)))

    (low, qkv, probs, context, unit1, hidden, active, slope, unit2, scale, out) = forward_chain(
        fresh, to_home(text[:, 0]), memory_rows, table, gathered
    )
    layer_out = from_home(disorder(out))
    (grad_qkv, grad_proj, grad_upper, grad_down, text_grad, narrow, wide, memory_grad) = (
        backward_chain(
            fresh, to_home(order(cotangent[:, 0])), table, qkv, probs, unit1, slope, unit2, scale,
            gathered,
        )
    )
    text_grad = from_home(text_grad).astype(F32)

    def flat(block, layer):
        return block[:, layer].reshape(-1, block.shape[-1])

    pieces = []
    for layer in range(2):
        for left, right in (
            (low, grad_qkv),
            (context, grad_proj),
            (hidden, grad_upper),
            (active, grad_down),
        ):
            full = dot(flat(left, layer), flat(right, layer), TN).astype(LOW)
            full = full.reshape(chain, full.shape[0] // chain, full.shape[1])
            for i in range(0, full.shape[2], width):
                pieces.append(full[:, :, i : i + width])
    matrices = lax.psum_scatter(
        jnp.concatenate(pieces, 1), "seg", scatter_dimension=0, tiled=True
    )[0]
    narrow = jnp.sum(narrow, 2)
    wide = jnp.sum(wide, 2)
    pieces = [memory_grad[:mem].reshape(mem, chain, part).swapaxes(0, 1).reshape(chain, -1)]
    for layer in range(2):
        gain2, shift2, down, gain1, shift1, out_bias, query, value = (
            narrow[layer, i] for i in range(8)
        )
        for v in (
            jnp.concatenate([query, value]), out_bias, gain1, shift1, wide[layer].reshape(-1), down,
            gain2, shift2,
        ):
            pieces.append(v.reshape(chain, -1))
    vectors = lax.psum_scatter(
        jnp.concatenate(pieces, 1).astype(LOW), "seg", scatter_dimension=0, tiled=True
    )[0]
    matrices, vectors = lax.psum((matrices, vectors), "item")
    matrices, vectors = matrices.astype(F32), vectors.astype(F32)

    results = []
    row, at = 0, mem * part
    for layer in range(2):
        shapes = [w.shape for w in layers[layer]]
        for shape in shapes:
            if len(shape) == 1:
                results.append(vectors[at : at + shape[0]])
                at += shape[0]
            else:
                blocks = []
                for _ in range(shape[1] // width):
                    blocks.append(matrices[row : row + shape[0]])
                    row += shape[0]
                results.append(jnp.concatenate(blocks, 1))
    return (
        layer_out[:, None],
        text_grad[:, None],
        vectors[: mem * part].reshape(mem, part),
        *results,
    )


def regroup(gathered, together, part):
    shards, total, width = gathered.shape
    blocks = gathered.reshape(shards // together, together, total // part, part, width)
    pieces = []
    for layer in range(2):
        base = layer * BLOCKS
        for block in range(8):
            pieces.append(blocks[:, :, base + block])
        pieces.append(blocks[:, :, base + 8 : base + 12])
    return jnp.concatenate(
        [p.reshape(shards // together, -1, width) for p in pieces], 1
    )


def solution(mesh):
    seg = (P("seg", None), P("seg"), P("seg", None)) + (P("seg"),) * 3
    seg = seg + (P("seg", None), P("seg"), P("seg", None)) + (P("seg"),) * 3
    rows = P("item", "seg", None, None)
    return jax.shard_map(
        body,
        mesh=mesh,
        in_specs=(rows, rows, P("item"), P()) + seg + seg,
        out_specs=(rows, rows, P(None, "seg")) + seg + seg,
        check_vma=False,
    )
```

```python
import jax
import jax.numpy as jnp
from jax import lax
from jax.experimental import pallas as pl
from jax.experimental.pallas import tpu as pltpu
from jax.sharding import PartitionSpec as P

HEAD_DIM = 64
EPSILON = 1e-05
F32 = jnp.float32
LOW = jnp.bfloat16
NN = (((1,), (0,)), ((), ()))
NT = (((1,), (1,)), ((), ()))
TN = (((0,), (0,)), ((), ()))

PAD = 16
BLOCKS = 12
B_QUERY, B_VALUE, B_OUT, GAIN1, SHIFT1, B_UP, B_DOWN, GAIN2, SHIFT2 = 0, 1, 2, 3, 4, 5, 9, 10, 11


def dot(left, right, dims=NN):
    return lax.dot_general(left, right, dims, preferred_element_type=F32)


def norm_rows(total, gain, shift):
    centre = total - jnp.mean(total, -1, keepdims=True)
    scale = lax.rsqrt(jnp.mean(centre * centre, -1, keepdims=True) + EPSILON)
    unit = centre * scale
    return unit, scale, unit * gain + shift


def norm_back(grad, unit, scale, gain):
    t = grad * gain
    return scale * (
        t - jnp.mean(t, -1, keepdims=True) - unit * jnp.mean(t * unit, -1, keepdims=True)
    )


def gelu_and_slope(upper):
    density = jnp.exp(upper * upper * -0.5) * 0.3989422804014327
    below = 0.5 * (1.0 + lax.erf(upper * 0.7071067811865476))
    return upper * below, below + upper * density


def fold(block):
    rows, width = block.shape
    return jnp.sum(block.reshape(rows // 8, 8, width), 0)


def two_heads(block, first):
    zero = jnp.zeros_like(block)
    return jnp.concatenate([jnp.where(first, block, zero), jnp.where(first, zero, block)], 0)


def copy_block(gathered, target, layer, block, part, sem):
    shards = gathered.shape[0]
    base = layer * BLOCKS * part

    def copy(shard, row, to, count):
        pltpu.make_async_copy(
            gathered.at[shard, pl.ds(pl.multiple_of(row, 16), count)],
            target(pl.multiple_of(to, 16), count),
            sem,
        ).start()

    @pl.when(block < 8)
    def _():
        def start(shard, none):
            copy(shard, base + block * part, shard * part, part)
            return none

        lax.fori_loop(0, shards, start, 0)

    @pl.when(block >= 8)
    def _():
        def start(i, none):
            shard = (block - 8) * (shards // 4) + i
            copy(shard, base + 8 * part, i * 4 * part, 4 * part)
            return none

        lax.fori_loop(0, shards // 4, start, 0)


def load_weights(gathered, held, width, sem):
    part = width // gathered.shape[0]

    def start(index, none):
        def target(row, count):
            return held.at[pl.ds(pl.multiple_of(index * width + row, 16), count)]

        copy_block(gathered, target, index // BLOCKS, index % BLOCKS, part, sem)
        return none

    lax.fori_loop(0, 2 * BLOCKS, start, 0)
    pltpu.make_async_copy(held, held, sem).wait()


def load_turned(gathered, held, stage, width, sems):
    part = width // gathered.shape[0]

    def start(index):
        slot = index % 2

        def target(row, count):
            return stage.at[slot, pl.ds(row, count)]

        copy_block(gathered, target, index // BLOCKS, index % BLOCKS, part, sems.at[slot])

    start(0)

    def turn(index, none):
        slot = index % 2

        @pl.when(index + 1 < 2 * BLOCKS)
        def _():
            start(index + 1)

        pltpu.make_async_copy(stage.at[slot], stage.at[slot], sems.at[slot]).wait()
        held[pl.ds(pl.multiple_of(index * width, width), width), :] = stage[slot].T
        return none

    lax.fori_loop(0, 2 * BLOCKS, turn, 0)


def split_refs(refs, sizes):
    parts = []
    for size in sizes:
        parts.append(refs[:size])
        refs = refs[size:]
    return parts


def forward_kernel(*refs):
    (
        (fresh_ref, text_ref, memory_ref, vector_ref, gathered_ref),
        low_ref, qkv_ref, probs_ref, context_ref, unit1_ref, hidden_ref, active_ref, slope_ref,
        unit2_ref,
        (scale_ref, out_ref, held, carry, sem),
    ) = split_refs(refs, [5] + [2] * 9 + [5])
    step = pl.program_id(0)
    texts, width = text_ref.shape[1:]
    rows = texts + 2 * PAD
    mem = 10

    @pl.when(step == 0)
    def _():
        load_weights(gathered_ref, held, width, sem)
        carry[...] = jnp.zeros_like(carry)

    column = lax.broadcasted_iota(jnp.int32, (2 * rows, rows), 1)
    unused = jnp.logical_or(
        column >= texts + PAD + mem,
        jnp.logical_and(column >= texts + mem, column < texts + PAD),
    )
    mask = jnp.where(unused, -1e30, 0.0).astype(F32)
    first_head = lax.broadcasted_iota(jnp.int32, (rows, 2 * HEAD_DIM), 1) < HEAD_DIM

    memory = memory_ref[...]
    read = jnp.where(fresh_ref[step] > 0, memory, carry[...])
    x = jnp.concatenate([text_ref[0], read, memory], 0).astype(F32)
    scales = []
    for index in range(2):

        def weight(block, index=index):
            return held[(index * BLOCKS + block) * width : (index * BLOCKS + block + 1) * width, :]

        def vector(row, index=index):
            return vector_ref[index, row : row + 1, :]

        low = x.astype(LOW)
        low_ref[index][0] = low
        query = (dot(low, weight(0)) + vector(B_QUERY)).astype(LOW)
        keys = dot(low, weight(1)).astype(LOW)
        values = (dot(low, weight(2)) + vector(B_VALUE)).astype(LOW)
        qkv_ref[index][0, :, :width] = query
        qkv_ref[index][0, :, width : 2 * width] = keys
        qkv_ref[index][0, :, 2 * width :] = values
        for pair in range(width // (2 * HEAD_DIM)):
            cols = slice(2 * HEAD_DIM * pair, 2 * HEAD_DIM * (pair + 1))
            scores = dot(two_heads(query[:, cols], first_head), keys[:, cols], NT)
            scores = scores * HEAD_DIM ** (-0.5) + mask
            weights = jnp.exp(scores - jnp.max(scores, -1, keepdims=True))
            probs = (weights / jnp.sum(weights, -1, keepdims=True)).astype(LOW)
            probs_ref[index][0, pair] = probs
            both = dot(probs, values[:, cols])
            context_ref[index][0, :, cols] = jnp.where(
                first_head, both[:rows], both[rows:]
            ).astype(LOW)
        total = x + dot(context_ref[index][0], weight(3)) + vector(B_OUT)
        unit, scale, hidden = norm_rows(total, vector(GAIN1), vector(SHIFT1))
        unit1_ref[index][0] = unit.astype(LOW)
        scales.append(scale)
        hidden_low = hidden.astype(LOW)
        hidden_ref[index][0] = hidden_low
        total = hidden + vector(B_DOWN)
        for block in range(4):
            cols = slice(block * width, (block + 1) * width)
            upper = dot(hidden_low, weight(4 + block)) + vector(B_UP + block)
            active, slope = gelu_and_slope(upper)
            active = active.astype(LOW)
            active_ref[index][0, :, cols] = active
            slope_ref[index][0, :, cols] = slope.astype(LOW)
            total = total + dot(active, weight(8 + block))
        unit, scale, x = norm_rows(total, vector(GAIN2), vector(SHIFT2))
        unit2_ref[index][0] = unit.astype(LOW)
        scales.append(scale)
    lane = lax.broadcasted_iota(jnp.int32, (rows, 128), 1)
    packed = scales[3]
    for i in (2, 1, 0):
        packed = jnp.where(lane < 32 * (i + 1), scales[i], packed)
    scale_ref[0] = packed
    final = x.astype(LOW)
    out_ref[0] = final
    carry[...] = final[texts + PAD :]


def backward_kernel(*refs):
    (
        (fresh_ref, cotangent_ref, vector_ref, scale_ref, gathered_ref),
        qkv_ref, probs_ref, unit1_ref, slope_ref, unit2_ref,
        grad_qkv_ref, grad_proj_ref, grad_upper_ref, grad_down_ref,
        (text_ref, narrow_ref, wide_ref, memory_ref, held, carry, stage, sems),
    ) = split_refs(refs, [5] + [2] * 5 + [2] * 4 + [8])
    turn = pl.program_id(0)
    step = pl.num_programs(0) - 1 - turn
    rows, width = cotangent_ref.shape[1:]
    texts = rows - 2 * PAD

    @pl.when(turn == 0)
    def _():
        load_turned(gathered_ref, held, stage, width, sems)
        carry[...] = jnp.zeros_like(carry)
        narrow_ref[...] = jnp.zeros_like(narrow_ref)
        wide_ref[...] = jnp.zeros_like(wide_ref)
        memory_ref[...] = jnp.zeros_like(memory_ref)

    first_head = lax.broadcasted_iota(jnp.int32, (rows, 2 * HEAD_DIM), 1) < HEAD_DIM
    grad = jnp.concatenate(
        [
            cotangent_ref[0, : texts + PAD].astype(F32),
            cotangent_ref[0, texts + PAD :].astype(F32) + carry[...].astype(F32),
        ],
        0,
    )
    for index in (1, 0):

        def weight(block, index=index):
            return held[(index * BLOCKS + block) * width : (index * BLOCKS + block + 1) * width, :]

        def vector(row, index=index):
            return vector_ref[index, row : row + 1, :]

        def scale(norm, index=index):
            lane = 32 * (2 * index + norm)
            return scale_ref[0, :, lane : lane + 1]

        unit = unit2_ref[index][0].astype(F32)
        narrow_ref[index, 0] += fold(grad * unit)
        narrow_ref[index, 1] += fold(grad)
        grad_second = norm_back(grad, unit, scale(1), vector(GAIN2))
        narrow_ref[index, 2] += fold(grad_second)
        grad_down = grad_second.astype(LOW)
        grad_hidden = grad_second
        for block in range(4):
            cols = slice(block * width, (block + 1) * width)
            grad_upper = dot(grad_down, weight(8 + block)) * slope_ref[index][0, :, cols].astype(F32)
            wide_ref[index, block] += fold(grad_upper)
            grad_upper = grad_upper.astype(LOW)
            grad_upper_ref[index][0, :, cols] = grad_upper
            grad_hidden = grad_hidden + dot(grad_upper, weight(4 + block))
        grad_down_ref[index][0] = grad_down
        unit = unit1_ref[index][0].astype(F32)
        narrow_ref[index, 3] += fold(grad_hidden * unit)
        narrow_ref[index, 4] += fold(grad_hidden)
        grad_first = norm_back(grad_hidden, unit, scale(0), vector(GAIN1))
        narrow_ref[index, 5] += fold(grad_first)
        grad_proj = grad_first.astype(LOW)
        grad_proj_ref[index][0] = grad_proj
        grad_context = dot(grad_proj, weight(3)).astype(LOW)
        for pair in range(width // (2 * HEAD_DIM)):
            cols = slice(2 * HEAD_DIM * pair, 2 * HEAD_DIM * (pair + 1))
            in_keys = slice(width + cols.start, width + cols.stop)
            in_values = slice(2 * width + cols.start, 2 * width + cols.stop)
            query = two_heads(qkv_ref[index][0, :, cols], first_head)
            keys = qkv_ref[index][0, :, in_keys]
            values = qkv_ref[index][0, :, in_values]
            context = two_heads(grad_context[:, cols], first_head)
            probs_low = probs_ref[index][0, pair]
            probs = probs_low.astype(F32)
            term = dot(context, values, NT) * probs
            grad_scores = term - probs * jnp.sum(term, -1, keepdims=True)
            grad_scores = (grad_scores * HEAD_DIM ** (-0.5)).astype(LOW)
            both = dot(grad_scores, keys)
            grad_query = jnp.where(first_head, both[:rows], both[rows:])
            grad_keys = dot(grad_scores, query, TN)
            grad_values = dot(probs_low, context, TN)
            narrow_ref[index, 6, :, cols] += fold(grad_query)
            narrow_ref[index, 7, :, cols] += fold(grad_values)
            grad_qkv_ref[index][0, :, cols] = grad_query.astype(LOW)
            grad_qkv_ref[index][0, :, in_keys] = grad_keys.astype(LOW)
            grad_qkv_ref[index][0, :, in_values] = grad_values.astype(LOW)
        grad = grad_first
        for block in range(3):
            cols = slice(block * width, (block + 1) * width)
            grad = grad + dot(grad_qkv_ref[index][0, :, cols], weight(block))
    text_ref[0] = grad[:texts].astype(LOW)
    read = grad[texts : texts + PAD]
    fresh = fresh_ref[step] > 0
    memory_ref[...] += grad[texts + PAD :] + jnp.where(fresh, read, 0.0)
    carry[...] = jnp.where(fresh, 0.0, read).astype(LOW)


SMEM = pl.BlockSpec(memory_space=pltpu.SMEM)
VMEM = pl.BlockSpec(memory_space=pltpu.VMEM)
ANY = pl.BlockSpec(memory_space=pl.ANY)


def cost(rows, width, segments):
    return pl.CostEstimate(
        flops=2 * rows * 2 * BLOCKS * width * width * segments * 4,
        bytes_accessed=2 * 2 * BLOCKS * width * width,
        transcendentals=0,
    )


def forward_chain(fresh, text, memory, vectors, gathered):
    segments, texts, width = text.shape
    rows = texts + 2 * PAD
    pairs = width // (2 * HEAD_DIM)

    def block(shape):
        return pl.BlockSpec((1,) + shape, lambda s: (s,) + (0,) * len(shape))

    row = (rows, width)
    shapes = [row, (rows, 3 * width), (pairs, 2 * rows, rows), row, row, row]
    shapes += [(rows, 4 * width), (rows, 4 * width), row]
    outs = [(shape, LOW) for shape in shapes for _ in range(2)]
    outs += [((rows, 128), F32), (row, LOW)]
    found = pl.pallas_call(
        forward_kernel,
        grid=(segments,),
        in_specs=[SMEM, block((texts, width)), VMEM, VMEM, ANY],
        out_specs=[block(shape) for shape, _ in outs],
        out_shape=[jax.ShapeDtypeStruct((segments,) + shape, kind) for shape, kind in outs],
        scratch_shapes=[
            pltpu.VMEM((2 * BLOCKS * width, width), LOW),
            pltpu.VMEM((PAD, width), LOW),
            pltpu.SemaphoreType.DMA,
        ],
        compiler_params=pltpu.CompilerParams(vmem_limit_bytes=62 << 20),
        cost_estimate=cost(rows, width, segments),
        name="forward_chain",
    )(fresh, text, memory, vectors, gathered)
    return split_refs(found, [2] * 9 + [1, 1])


def backward_chain(fresh, cotangent, vectors, scale, saved, gathered):
    segments, rows, width = cotangent.shape
    texts = rows - 2 * PAD
    pairs = width // (2 * HEAD_DIM)

    def block(shape):
        return pl.BlockSpec((1,) + shape, lambda t: (segments - 1 - t,) + (0,) * len(shape))

    row, three, four = (rows, width), (rows, 3 * width), (rows, 4 * width)
    outs = [shape for shape in (three, row, four, row) for _ in range(2)] + [(texts, width)]
    ins = [shape for shape in (three, (pairs, 2 * rows, rows), row, four, row) for _ in range(2)]
    found = pl.pallas_call(
        backward_kernel,
        grid=(segments,),
        in_specs=[SMEM, block(row), VMEM, block((rows, 128)), ANY]
        + [block(shape) for shape in ins],
        out_specs=[block(shape) for shape in outs] + [VMEM, VMEM, VMEM],
        out_shape=[jax.ShapeDtypeStruct((segments,) + shape, LOW) for shape in outs]
        + [
            jax.ShapeDtypeStruct((2, 8, 8, width), F32),
            jax.ShapeDtypeStruct((2, 4, 8, width), F32),
            jax.ShapeDtypeStruct((PAD, width), F32),
        ],
        scratch_shapes=[
            pltpu.VMEM((2 * BLOCKS * width, width), LOW),
            pltpu.VMEM((PAD, width), LOW),
            pltpu.VMEM((2, width, width), LOW),
            pltpu.SemaphoreType.DMA((2,)),
        ],
        input_output_aliases={5: 0, 6: 1, 9: 2, 10: 3, 11: 4, 12: 5, 13: 6, 14: 7},
        compiler_params=pltpu.CompilerParams(vmem_limit_bytes=62 << 20),
        cost_estimate=cost(rows, width, segments),
        name="backward_chain",
    )(fresh, cotangent, vectors, scale, gathered, *(a for pair in saved for a in pair))
    return split_refs(found, [2] * 4 + [1] * 4)


def split_columns(shard, width):
    rows, columns = shard.shape
    return [shard[:, i : i + width] for i in range(0, columns, width)]


class Slice:
    def __init__(self, micro):
        self.micro, self.half = micro, micro // 2
        self.bits = self.half.bit_length() - 1
        self.chain, self.items = lax.axis_size("seg"), lax.axis_size("item")
        self.start = (self.chain - 2 * micro) // 2
        self.place, self.item = lax.axis_index("seg"), lax.axis_index("item")
        self.core = self.place % 2
        self.home = jnp.clip((self.place - self.start) // 2, 0, micro - 1)
        self.high, self.low = self.home // self.half, self.home % self.half
        self.at_home = jnp.logical_and(
            self.place >= self.start, self.place < self.start + 2 * micro
        )

    def seat(self, home, core=0):
        return self.start + 2 * home + core

    def far(self, home, core=0):
        return self.seat(home, core) + self.micro * (-1 if home < self.half else 1)

    def send(self, value, pairs):
        flat = [(a * self.items + x, b * self.items + x) for a, b in pairs for x in range(self.items)]
        return lax.ppermute(value, ("seg", "item"), flat)

    def send_across(self, value, bit):
        flat = []
        for i in range(self.micro):
            for c in range(2):
                at = self.seat(i, c) * self.items
                flat += [(at + x, at + (x ^ (1 << bit))) for x in range(self.items)]
        return lax.ppermute(value, ("seg", "item"), flat)

    def between_homes(self, flip):
        return [(self.seat(i, c), self.seat(i ^ flip, c)) for i in range(self.micro) for c in range(2)]

    def in_order(self, mine, got, side, axis):
        return jnp.where(
            side == 0, jnp.stack([mine, got], axis), jnp.stack([got, mine], axis)
        )

    def joined(self, mine, got, side, axis):
        return jnp.where(
            side == 0, jnp.concatenate([mine, got], axis), jnp.concatenate([got, mine], axis)
        )

    def gather(self, value, items=False):
        homes = [(i, c) for i in range(self.micro) for c in range(2)]
        got = self.send(value, [(self.far(i, c), self.seat(i, c)) for i, c in homes])
        whole = self.in_order(value, got, 1 - self.high, 0)
        if items:
            whole = whole.reshape((2,) + (2,) * (1 + self.bits) + value.shape[1:])
        whole = whole.reshape((1,) * (1 + self.bits) + whole.shape)
        for bit in range(self.bits + 1):
            axis = self.bits - bit
            side = (self.home >> bit) % 2
            out = whole
            if items:
                at = 2 + self.bits + axis
                out = lax.dynamic_index_in_dim(whole, 1 - side, at, keepdims=True)
                whole = lax.dynamic_index_in_dim(whole, side, at, keepdims=True)
            whole = self.joined(whole, self.send(out, self.between_homes(1 << bit)), side, axis)
        rest = value.shape[1:] if items else value.shape
        whole = whole.reshape((2, self.half, 2) + rest).swapaxes(1, 2)
        got = self.send(whole, [(self.seat(i, c), self.seat(i, 1 - c)) for i, c in homes])
        return self.in_order(whole, got, self.core, 3).reshape((self.chain,) + rest)

    def spread(self, value, waits):
        rest = value.shape[1:]
        whole = value.reshape((2, 2, self.half, 2) + rest)
        whole = lax.dynamic_index_in_dim(whole, self.core, 3, keepdims=False).swapaxes(1, 2)
        whole = whole.reshape((2,) * (1 + self.bits) + (1,) * (1 + self.bits) + (2,) + rest)
        for bit in reversed(range(self.bits + 1)):
            axis = self.bits - bit
            side = (self.home >> bit) % 2
            wait = waits[min(axis, len(waits) - 1)]
            got = self.send(
                lax.dynamic_index_in_dim(whole, 1 - side + wait, axis, keepdims=True),
                self.between_homes(1 << bit),
            )
            whole = lax.dynamic_index_in_dim(whole, side, axis, keepdims=True)
            wait = waits[min(axis + 1, len(waits) - 1)]
            whole = self.joined(whole, got, side + wait, 1 + self.bits + axis)
        whole = whole.reshape((self.micro, 2) + rest)
        near = lax.dynamic_index_in_dim(whole, 1 - self.high, 1, keepdims=False)
        away = lax.dynamic_index_in_dim(whole, self.high + waits[-1], 1, keepdims=False)
        homes = [(i, c) for i in range(self.micro) for c in range(2)]
        got = self.send(away, [(self.seat(i, c), self.far(i, c)) for i, c in homes])
        return jnp.where(self.at_home, near, got)

    def halvings(self, order):
        stages = []
        for name in order:
            if name == "x":
                stages += [("x", b) for b in range(self.items.bit_length() - 1)]
            elif name == "h":
                stages.append(("h", self.bits))
            else:
                stages += [("l", b) for b in range(self.bits)]
        return stages

    def halve(self, terms, stage, wait):
        name, bit = stage
        side = ((self.item if name == "x" else self.home) >> bit) % 2
        axis = {"x": -1, "h": 0, "l": 1 + self.bits - bit}[name]

        def cut(term, side):
            found = []
            for f in term:
                size = f.shape[axis] // 2
                found.append(lax.dynamic_slice_in_dim(f, side * size, size, axis))
            return found[0] if len(found) == 1 else jnp.concatenate(found, -1)

        out = add([cut(t, 1 - side + wait) for t in terms])
        if name == "x":
            got = self.send_across(out, bit)
        else:
            got = self.send(out, self.between_homes(1 << bit))
        return out, [[cut(t, side)] for t in terms] + [[got]]

    def deliver(self, total):
        near = lax.dynamic_index_in_dim(total, 1 - self.high, 0, keepdims=False)
        away = lax.dynamic_index_in_dim(total, self.high, 0, keepdims=False)

        def of(pair, core):
            return lax.dynamic_index_in_dim(pair, core, 0, keepdims=False)

        homes = [(i, c) for i in range(self.micro) for c in range(2)]
        beside = self.send(
            of(near, 1 - self.core), [(self.seat(i, c), self.seat(i, 1 - c)) for i, c in homes]
        )
        straight = self.send(
            of(away, self.core), [(self.seat(i, c), self.far(i, c)) for i, c in homes]
        )
        crossed = self.send(
            of(away, 1 - self.core), [(self.seat(i, c), self.far(i, 1 - c)) for i, c in homes]
        )
        same = jnp.where(self.at_home, of(near, self.core), straight)
        both = self.in_order(same, beside + crossed, self.core, 0)
        if self.items == 2:
            swapped = lax.ppermute(both, "item", [(0, 1), (1, 0)])
            return [
                jnp.where(self.item == 0, both, swapped),
                jnp.where(self.item == 0, swapped, both),
            ]
        every = lax.all_gather(both, "item")
        width = self.items.bit_length() - 1
        return [every[int(format(x, "0%db" % width)[::-1], 2)] for x in range(self.items)]

    def reduce(self, chunks, text, out):
        kind = (2, 2) + (2,) * self.bits + (2,)
        terms = [[[f.reshape(kind + f.shape[1:]) for f in fulls]] for fulls, _ in chunks]
        stages = [self.halvings(order) for _, order in chunks]
        wait, waits = 0, []
        for turn in range(len(stages[0])):
            outs = []
            for i in range(len(chunks)):
                sent, terms[i] = self.halve(terms[i], stages[i][turn], wait)
                outs.append(sent)
            wait = after(outs[-1])
            waits.append(wait)
        text = self.spread(text, waits).astype(F32)
        out = self.spread(out, [0] + waits[1:])
        rows = min(f.shape[1] for fulls, _ in chunks for f in fulls)
        totals = []
        for t in terms:
            total = add([f[0] for f in t])
            total = total.reshape((2, 2) + total.shape[-2:])
            strips = [total[:, :, i : i + rows] for i in range(0, total.shape[2], rows)]
            totals.append(strips[0] if len(strips) == 1 else jnp.concatenate(strips, -1))
        found = []
        for group in ((0, 1), (2,)):
            sides = self.deliver(jnp.concatenate([totals[i] for i in group], -1))
            at = 0
            for i in group:
                for f in chunks[i][0]:
                    size = f.shape[2] // self.items
                    strips = []
                    for _ in range(f.shape[1] // rows):
                        strips.append(
                            jnp.concatenate([side[..., at : at + size] for side in sides], -1)
                        )
                        at += size
                    found.append(jnp.concatenate(strips, 1).astype(F32))
        return found, text, out


def after(*values):
    zero = jnp.int32(0)
    for v in values:
        one = v[(0,) * v.ndim]
        zero = zero + (one != one).astype(jnp.int32)
    return zero


def add(terms):
    total = terms[0].astype(F32)
    for t in terms[1:]:
        total = total + t.astype(F32)
    return total.astype(LOW)


def body(text, cotangent, unroll, memory, *weights):
    micro, _, texts, width = text.shape
    mem = memory.shape[0]
    chain = lax.axis_size("seg")
    part = width // chain
    layers = (weights[:12], weights[12:])
    net = Slice(micro)

    def order(block):
        zero = jnp.zeros((block.shape[0], PAD - mem, width), block.dtype)
        return jnp.concatenate(
            [block[:, mem : mem + texts], block[:, :mem], zero, block[:, mem + texts :], zero], 1
        )

    def disorder(block):
        return jnp.concatenate(
            [
                block[:, texts : texts + mem],
                block[:, :texts],
                block[:, texts + PAD : texts + PAD + mem],
            ],
            1,
        )

    shards = []
    for w in layers:
        for matrix in (w[0], w[2], w[6], w[8]):
            shards += split_columns(matrix, width)
    gathered = lax.all_gather(jnp.concatenate(shards), "seg")
    if part % 16:
        gathered = regroup(gathered, 16 // (part & -part), part)
    text_home = net.gather(text[:, 0], items=True)
    cotangent_home = order(net.gather(cotangent[:, 0], items=True))
    vectors = jnp.concatenate([v for w in layers for v in w if v.ndim == 1])
    vectors = net.gather(vectors.reshape(-1, 2 * BLOCKS * part // 8)).reshape(chain, -1)
    vectors = vectors.astype(F32)
    rows_of = []
    at = 0
    for w in layers:
        for v in w:
            if v.ndim == 1:
                rows_of.append(vectors[:, at : at + v.shape[0]].reshape(-1, width))
                at += v.shape[0]
    half = len(rows_of) // 2
    table = jnp.stack([jnp.concatenate(rows_of[:half]), jnp.concatenate(rows_of[half:])])
    table = jnp.pad(table, ((0, 0), (0, 16 - table.shape[1]), (0, 0)))

    limit = unroll[net.home]
    segments = jnp.arange(chain, dtype=jnp.int32)
    fresh = jnp.logical_or(segments == 0, segments == limit).astype(jnp.int32)
    memory_rows = jnp.pad(memory, ((0, PAD - mem), (0, 0)))

    (low, qkv, probs, context, unit1, hidden, active, slope, unit2, (scale,), (out,)) = (
        forward_chain(fresh, text_home, memory_rows, table, gathered)
    )
    (grad_qkv, grad_proj, grad_upper, grad_down, (text_grad,), (narrow,), (wide,), (memory_grad,)) = (
        backward_chain(
            fresh, cotangent_home, table, scale,
            (qkv, probs, unit1, slope, unit2), gathered,
        )
    )

    def own_layer(pair):
        mine = jnp.where(net.core == 0, *pair)
        return mine.reshape(-1, mine.shape[-1])

    def product(left, right):
        full = dot(own_layer(left), own_layer(right), TN).astype(LOW)
        return full.reshape(chain, full.shape[0] // chain, full.shape[1])

    def vector_terms():
        sums, wides = jnp.sum(narrow, 2), jnp.sum(wide, 2)
        terms = [memory_grad[:mem].reshape(mem, chain, part).swapaxes(0, 1).reshape(chain, -1)]
        for layer in range(2):
            gain2, shift2, down, gain1, shift1, out_bias, query, value = (
                sums[layer, i] for i in range(8)
            )
            for v in (
                jnp.concatenate([query, value]), out_bias, gain1, shift1, wides[layer].reshape(-1),
                down, gain2, shift2,
            ):
                terms.append(v.reshape(chain, -1))
        terms = jnp.concatenate(terms, 1)
        terms = jnp.where(net.core == 0, terms, 0.0).astype(LOW)
        terms = jnp.pad(terms, ((0, 0), (0, 256 * part - terms.shape[1])))
        return terms.reshape(chain, part, 256)

    (down, up, qkv, proj, terms), text_grad, layer_out = net.reduce(
        [
            ([product(active, grad_down)], "lhx"),
            ([product(hidden, grad_upper)], "hlx"),
            ([product(low, grad_qkv), product(context, grad_proj), vector_terms()], "xlh"),
        ],
        text_grad,
        disorder(out),
    )
    vectors = terms[0].reshape(-1)
    results = []
    at = mem * part
    for layer in range(2):
        left = [qkv[layer], proj[layer], up[layer], down[layer]]
        for w in layers[layer]:
            if w.ndim == 1:
                results.append(vectors[at : at + w.shape[0]])
                at += w.shape[0]
            else:
                results.append(left.pop(0))
    return (
        layer_out[:, None],
        text_grad[:, None],
        vectors[: mem * part].reshape(mem, part),
        *results,
    )


def regroup(gathered, together, part):
    shards, total, width = gathered.shape
    blocks = gathered.reshape(shards // together, together, total // part, part, width)
    pieces = []
    for layer in range(2):
        base = layer * BLOCKS
        for block in range(8):
            pieces.append(blocks[:, :, base + block])
        pieces.append(blocks[:, :, base + 8 : base + 12])
    return jnp.concatenate([p.reshape(shards // together, -1, width) for p in pieces], 1)


def solution(mesh):
    seg = (P("seg", None), P("seg"), P("seg", None)) + (P("seg"),) * 3
    seg = seg + (P("seg", None), P("seg"), P("seg", None)) + (P("seg"),) * 3
    rows = P("item", "seg", None, None)
    return jax.shard_map(
        body,
        mesh=mesh,
        in_specs=(rows, rows, P("item"), P()) + seg + seg,
        out_specs=(rows, rows, P(None, "seg")) + seg + seg,
        check_vma=False,
    )
```

```python
import functools

import jax
import jax.numpy as jnp
from jax import lax
from jax.experimental import pallas as pl
from jax.experimental.pallas import tpu as pltpu
from jax.sharding import PartitionSpec as P

HEAD_DIM = 64
EPSILON = 1e-05
F32 = jnp.float32
LOW = jnp.bfloat16
NN = (((1,), (0,)), ((), ()))
NT = (((1,), (1,)), ((), ()))
TN = (((0,), (0,)), ((), ()))

PAD = 16
BLOCKS = 12
B_QUERY, B_VALUE, B_OUT, GAIN1, SHIFT1, B_UP, B_DOWN, GAIN2, SHIFT2 = 0, 1, 2, 3, 4, 5, 9, 10, 11


def dot(left, right, dims=NN):
    return lax.dot_general(left, right, dims, preferred_element_type=F32)


def norm_rows(total, gain, shift):
    centre = total - jnp.mean(total, -1, keepdims=True)
    scale = lax.rsqrt(jnp.mean(centre * centre, -1, keepdims=True) + EPSILON)
    unit = centre * scale
    return unit, scale, unit * gain + shift


def norm_back(grad, unit, scale, gain):
    t = grad * gain
    return scale * (
        t - jnp.mean(t, -1, keepdims=True) - unit * jnp.mean(t * unit, -1, keepdims=True)
    )


def gelu_and_slope(upper):
    density = jnp.exp(upper * upper * -0.5) * 0.3989422804014327
    below = 0.5 * (1.0 + lax.erf(upper * 0.7071067811865476))
    return upper * below, below + upper * density


def fold(block):
    rows, width = block.shape
    return jnp.sum(block.reshape(rows // 8, 8, width), 0)


def two_heads(block, first):
    zero = jnp.zeros_like(block)
    return jnp.concatenate([jnp.where(first, block, zero), jnp.where(first, zero, block)], 0)


def copy_block(gathered, target, layer, block, part, sem):
    shards = gathered.shape[0]
    base = layer * BLOCKS * part

    def copy(shard, row, to, count):
        pltpu.make_async_copy(
            gathered.at[shard, pl.ds(pl.multiple_of(row, 16), count)],
            target(pl.multiple_of(to, 16), count),
            sem,
        ).start()

    @pl.when(block < 8)
    def _():
        def start(shard, none):
            copy(shard, base + block * part, shard * part, part)
            return none

        lax.fori_loop(0, shards, start, 0)

    @pl.when(block >= 8)
    def _():
        def start(i, none):
            shard = (block - 8) * (shards // 4) + i
            copy(shard, base + 8 * part, i * 4 * part, 4 * part)
            return none

        lax.fori_loop(0, shards // 4, start, 0)


def block_of(held, index, width):
    return held.at[pl.ds(pl.multiple_of(index * width, 128), width), :]


def start_weights(gathered, held, width, sems):
    part = width // gathered.shape[0]

    def start(index, none):
        def target(row, count):
            return held.at[pl.ds(pl.multiple_of(index * width + row, 16), count)]

        copy_block(gathered, target, index // BLOCKS, index % BLOCKS, part, sems.at[index])
        return none

    lax.fori_loop(0, 2 * BLOCKS, start, 0)


def start_turned(turned, held, width, sems):
    lanes = width // 128
    per = lanes + lanes // 2
    for index in reversed(range(2 * BLOCKS)):
        for lane in range(lanes):
            block, k = divmod(index * lanes + lane, per)
            for rows, at, part in parts_of(k, width):
                pltpu.make_async_copy(
                    turned.at[block, rows, at : at + 128],
                    held.at[
                        index * width + part.start : index * width + part.stop,
                        128 * lane : 128 * (lane + 1),
                    ],
                    sems.at[index],
                ).start()


def wait_block(held, index, width, sems):
    target = block_of(held, index, width)
    pltpu.make_async_copy(target, target, sems.at[index]).wait()


def split_refs(refs, sizes):
    parts = []
    for size in sizes:
        parts.append(refs[:size])
        refs = refs[size:]
    return parts


def forward_kernel(*refs):
    (
        (fresh_ref, text_ref, memory_ref, vector_ref, gathered_ref),
        low_ref, qkv_ref, probs_ref, context_ref, unit1_ref, hidden_ref, active_ref, slope_ref,
        unit2_ref,
        (scale_ref, out_ref, turned_ref, held, carry, sems),
    ) = split_refs(refs, [5] + [2] * 9 + [6])
    step = pl.program_id(0)
    texts, width = text_ref.shape[1:]
    rows = texts + 2 * PAD
    mem = 10
    first_head = lax.broadcasted_iota(jnp.int32, (rows, 2 * HEAD_DIM), 1) < HEAD_DIM

    def run():
        column = lax.broadcasted_iota(jnp.int32, (2 * rows, rows), 1)
        unused = jnp.logical_or(
            column >= texts + PAD + mem,
            jnp.logical_and(column >= texts + mem, column < texts + PAD),
        )
        mask = jnp.where(unused, -1e30, 0.0).astype(F32)
        memory = memory_ref[...]
        read = jnp.where(fresh_ref[step] > 0, memory, carry[...])
        x = jnp.concatenate([text_ref[0], read, memory], 0).astype(F32)
        scales = []
        for index in range(2):

            def weight(block, index=index):
                at = index * BLOCKS + block
                return held[at * width : (at + 1) * width, :]

            def vector(row, index=index):
                return vector_ref[index, row : row + 1, :]

            low = x.astype(LOW)
            low_ref[index][0] = low
            query = (dot(low, weight(0)) + vector(B_QUERY)).astype(LOW)
            keys = dot(low, weight(1)).astype(LOW)
            values = (dot(low, weight(2)) + vector(B_VALUE)).astype(LOW)
            qkv_ref[index][0, :, :width] = query
            qkv_ref[index][0, :, width : 2 * width] = keys
            qkv_ref[index][0, :, 2 * width :] = values
            query = query * LOW(HEAD_DIM ** (-0.5))
            pairs = range(width // (2 * HEAD_DIM))
            cols = [slice(2 * HEAD_DIM * p, 2 * HEAD_DIM * (p + 1)) for p in pairs]
            scores = [dot(two_heads(query[:, c], first_head), keys[:, c], NT) + mask for c in cols]
            weights = [jnp.exp(e - jnp.max(e, -1, keepdims=True)) for e in scores]
            totals = [jnp.sum(e, -1, keepdims=True) for e in weights]
            both = [dot(weights[p].astype(LOW), values[:, cols[p]]) for p in pairs]
            for p in pairs:
                inverse = 1.0 / totals[p]
                context = both[p] * inverse
                probs_ref[index][0, p] = (weights[p] * inverse).astype(LOW)
                context_ref[index][0, :, cols[p]] = jnp.where(
                    first_head, context[:rows], context[rows:]
                ).astype(LOW)
            total = x + dot(context_ref[index][0], weight(3)) + vector(B_OUT)
            unit, scale, hidden = norm_rows(total, vector(GAIN1), vector(SHIFT1))
            unit1_ref[index][0] = unit.astype(LOW)
            scales.append(scale)
            hidden_low = hidden.astype(LOW)
            hidden_ref[index][0] = hidden_low
            total = hidden + vector(B_DOWN)
            upper = [dot(hidden_low, weight(4 + b)) + vector(B_UP + b) for b in range(4)]
            for block in range(4):
                wide = slice(block * width, (block + 1) * width)
                active, slope = gelu_and_slope(upper[block])
                active = active.astype(LOW)
                active_ref[index][0, :, wide] = active
                slope_ref[index][0, :, wide] = slope.astype(LOW)
                total = total + dot(active, weight(8 + block))
            unit, scale, x = norm_rows(total, vector(GAIN2), vector(SHIFT2))
            unit2_ref[index][0] = unit.astype(LOW)
            scales.append(scale)
        lane = lax.broadcasted_iota(jnp.int32, (rows, 128), 1)
        packed = scales[3]
        for i in (2, 1, 0):
            packed = jnp.where(lane < 32 * (i + 1), scales[i], packed)
        scale_ref[0] = packed
        final = x.astype(LOW)
        out_ref[0] = final
        carry[...] = final[texts + PAD :]

    @pl.when(step == 0)
    def _():
        start_weights(gathered_ref, held, width, sems)
        for block in range(2 * BLOCKS):
            wait_block(held, block, width, sems)
        carry[...] = jnp.zeros_like(carry)

    run()

    steps = turns_of(pl.num_programs(0))
    lanes = width // 128
    per = lanes + lanes // 2

    def turn(k):
        row = pl.multiple_of(((step // steps) * per + k) * 128, 128)
        strip = held[pl.ds(row, 128), :].T
        for rows, at, part in parts_of(k, width):
            turned_ref[0, rows, at : at + 128] = strip[part]

    for k in range(per):
        if steps == 1:
            turn(k)
        else:
            pl.when(step % steps == k % steps)(functools.partial(turn, k))


def parts_of(k, width):
    lanes = width // 128
    if k < lanes:
        return [(slice(0, width), 128 * k, slice(0, width))]
    half, at = width // 2, 256 * (k - lanes)
    return [
        (slice(width, width + half), at + 128 * i, slice(half * i, half * (i + 1))) for i in range(2)
    ]


def turns_of(segments):
    return max(segments // 16, 1)


def backward_kernel(*refs):
    (
        (fresh_ref, cotangent_ref, vector_ref, scale_ref, turned_ref),
        qkv_ref, probs_ref, unit1_ref, slope_ref, unit2_ref,
        grad_qkv_ref, grad_proj_ref, grad_upper_ref, grad_down_ref,
        (text_ref, table_ref, narrow_ref, wide_ref, memory_ref, held, carry, sems),
    ) = split_refs(refs, [5] + [2] * 5 + [2] * 4 + [8])
    turn = pl.program_id(0)
    step = pl.num_programs(0) - 1 - turn
    rows, width = cotangent_ref.shape[1:]
    texts = rows - 2 * PAD
    first_head = lax.broadcasted_iota(jnp.int32, (rows, 2 * HEAD_DIM), 1) < HEAD_DIM

    def run(loading):
        grad = cotangent_ref[0].astype(F32)
        if not loading:
            grad = jnp.concatenate(
                [grad[: texts + PAD], grad[texts + PAD :] + carry[...].astype(F32)], 0
            )
        for index in (1, 0):

            def weight(block, index=index):
                at = index * BLOCKS + block
                if loading:
                    wait_block(held, at, width, sems)
                return held[at * width : (at + 1) * width, :]

            def vector(row, index=index):
                return vector_ref[index, row : row + 1, :]

            def scale(norm, index=index):
                lane = 32 * (2 * index + norm)
                return scale_ref[0, :, lane : lane + 1]

            unit = unit2_ref[index][0].astype(F32)
            narrow_ref[index, 0] += fold(grad * unit)
            narrow_ref[index, 1] += fold(grad)
            grad_second = norm_back(grad, unit, scale(1), vector(GAIN2))
            narrow_ref[index, 2] += fold(grad_second)
            grad_down = grad_second.astype(LOW)
            grad_hidden = grad_second
            ahead = dot(grad_down, weight(11))
            for block in (3, 2, 1, 0):
                wide = slice(block * width, (block + 1) * width)
                grad_upper = ahead * slope_ref[index][0, :, wide].astype(F32)
                if block:
                    ahead = dot(grad_down, weight(7 + block))
                wide_ref[index, block] += fold(grad_upper)
                grad_upper = grad_upper.astype(LOW)
                grad_upper_ref[index][0, :, wide] = grad_upper
                grad_hidden = grad_hidden + dot(grad_upper, weight(4 + block))
            grad_down_ref[index][0] = grad_down
            unit = unit1_ref[index][0].astype(F32)
            narrow_ref[index, 3] += fold(grad_hidden * unit)
            narrow_ref[index, 4] += fold(grad_hidden)
            grad_first = norm_back(grad_hidden, unit, scale(0), vector(GAIN1))
            narrow_ref[index, 5] += fold(grad_first)
            grad_proj = grad_first.astype(LOW)
            grad_proj_ref[index][0] = grad_proj
            grad_context = dot(grad_proj, weight(3)).astype(LOW)
            eighth = LOW(HEAD_DIM ** (-0.5))
            pairs = range(width // (2 * HEAD_DIM))
            cols = [slice(2 * HEAD_DIM * p, 2 * HEAD_DIM * (p + 1)) for p in pairs]
            in_keys = [slice(width + c.start, width + c.stop) for c in cols]
            in_values = [slice(2 * width + c.start, 2 * width + c.stop) for c in cols]
            query = [two_heads(qkv_ref[index][0, :, c] * eighth, first_head) for c in cols]
            context = [two_heads(grad_context[:, c], first_head) for c in cols]
            term = [dot(context[p], qkv_ref[index][0, :, in_values[p]], NT) for p in pairs]
            probs = [probs_ref[index][0, p] for p in pairs]
            term = [term[p] * probs[p].astype(F32) for p in pairs]
            total = [jnp.sum(t, -1, keepdims=True) for t in term]
            grad_scores = [(term[p] - probs[p].astype(F32) * total[p]).astype(LOW) for p in pairs]
            both = [dot(grad_scores[p], qkv_ref[index][0, :, in_keys[p]] * eighth) for p in pairs]
            grad_query = [jnp.where(first_head, b[:rows], b[rows:]) for b in both]
            grad_keys = [dot(grad_scores[p], query[p], TN) for p in pairs]
            grad_values = [dot(probs[p], context[p], TN) for p in pairs]
            for p in pairs:
                narrow_ref[index, 6, :, cols[p]] += fold(grad_query[p])
                narrow_ref[index, 7, :, cols[p]] += fold(grad_values[p])
                grad_qkv_ref[index][0, :, cols[p]] = grad_query[p].astype(LOW)
                grad_qkv_ref[index][0, :, in_keys[p]] = grad_keys[p].astype(LOW)
                grad_qkv_ref[index][0, :, in_values[p]] = grad_values[p].astype(LOW)
            grad = grad_first
            for block in (2, 1, 0):
                cols = slice(block * width, (block + 1) * width)
                grad = grad + dot(grad_qkv_ref[index][0, :, cols], weight(block))
        text_ref[0] = grad[:texts].astype(LOW)
        read = grad[texts : texts + PAD]
        fresh = fresh_ref[step] > 0
        memory_ref[...] += grad[texts + PAD :] + jnp.where(fresh, read, 0.0)
        carry[...] = jnp.where(fresh, 0.0, read).astype(LOW)

    @pl.when(turn == 0)
    def _():
        start_turned(turned_ref, held, width, sems)
        narrow_ref[...] = jnp.zeros_like(narrow_ref)
        wide_ref[...] = jnp.zeros_like(wide_ref)
        memory_ref[...] = jnp.zeros_like(memory_ref)
        run(True)

    @pl.when(turn > 0)
    def _():
        run(False)

    @pl.when(step == 0)
    def _():
        sums = [jnp.sum(narrow_ref[i, j], 0, keepdims=True) for i in range(2) for j in range(8)]
        sums += [jnp.sum(wide_ref[i, j], 0, keepdims=True) for i in range(2) for j in range(4)]
        table_ref[...] = jnp.concatenate(sums + [memory_ref[...]], 0)


SMEM = pl.BlockSpec(memory_space=pltpu.SMEM)
VMEM = pl.BlockSpec(memory_space=pltpu.VMEM)
ANY = pl.BlockSpec(memory_space=pl.ANY)


def cost(rows, width, segments):
    return pl.CostEstimate(
        flops=2 * rows * 2 * BLOCKS * width * width * segments * 4,
        bytes_accessed=2 * 2 * BLOCKS * width * width,
        transcendentals=0,
    )


def forward_chain(fresh, text, memory, vectors, gathered):
    segments, texts, width = text.shape
    rows = texts + 2 * PAD
    pairs = width // (2 * HEAD_DIM)

    def block(shape):
        return pl.BlockSpec((1,) + shape, lambda s: (s,) + (0,) * len(shape))

    row = (rows, width)
    shapes = [row, (rows, 3 * width), (pairs, 2 * rows, rows), row, row, row]
    shapes += [(rows, 4 * width), (rows, 4 * width), row]
    outs = [(shape, LOW) for shape in shapes for _ in range(2)]
    outs += [((rows, 128), F32), (row, LOW)]
    steps = turns_of(segments)
    found = pl.pallas_call(
        forward_kernel,
        grid=(segments,),
        in_specs=[SMEM, block((texts, width)), VMEM, VMEM, ANY],
        out_specs=[block(shape) for shape, _ in outs]
        + [pl.BlockSpec((1,) + gathered.shape[1:], lambda s: (s // steps, 0, 0))],
        out_shape=[jax.ShapeDtypeStruct((segments,) + shape, kind) for shape, kind in outs]
        + [jax.ShapeDtypeStruct(gathered.shape, LOW)],
        input_output_aliases={4: len(outs)} if steps > 1 else {},
        scratch_shapes=[
            pltpu.VMEM((2 * BLOCKS * width, width), LOW),
            pltpu.VMEM((PAD, width), LOW),
            pltpu.SemaphoreType.DMA((2 * BLOCKS,)),
        ],
        compiler_params=pltpu.CompilerParams(vmem_limit_bytes=62 << 20),
        cost_estimate=cost(rows, width, segments),
        name="forward_chain",
    )(fresh, text, memory, vectors, gathered)
    return split_refs(found, [2] * 9 + [1, 1, 1])


def backward_chain(fresh, cotangent, vectors, scale, saved, turned):
    segments, rows, width = cotangent.shape
    texts = rows - 2 * PAD
    pairs = width // (2 * HEAD_DIM)

    def block(shape):
        return pl.BlockSpec((1,) + shape, lambda t: (segments - 1 - t,) + (0,) * len(shape))

    row, three, four = (rows, width), (rows, 3 * width), (rows, 4 * width)
    outs = [shape for shape in (three, row, four, row) for _ in range(2)] + [(texts, width)]
    ins = [shape for shape in (three, (pairs, 2 * rows, rows), row, four, row) for _ in range(2)]
    found = pl.pallas_call(
        backward_kernel,
        grid=(segments,),
        in_specs=[SMEM, block(row), VMEM, block((rows, 128)), ANY]
        + [block(shape) for shape in ins],
        out_specs=[block(shape) for shape in outs] + [VMEM],
        out_shape=[jax.ShapeDtypeStruct((segments,) + shape, LOW) for shape in outs]
        + [jax.ShapeDtypeStruct((24 + PAD, width), F32)],
        scratch_shapes=[
            pltpu.VMEM((2, 8, 8, width), F32),
            pltpu.VMEM((2, 4, 8, width), F32),
            pltpu.VMEM((PAD, width), F32),
            pltpu.VMEM((2 * BLOCKS * width, width), LOW),
            pltpu.VMEM((PAD, width), LOW),
            pltpu.SemaphoreType.DMA((2 * BLOCKS,)),
        ],
        input_output_aliases={5: 0, 6: 1, 9: 2, 10: 3, 11: 4, 12: 5, 13: 6, 14: 7},
        compiler_params=pltpu.CompilerParams(vmem_limit_bytes=62 << 20),
        cost_estimate=cost(rows, width, segments),
        name="backward_chain",
    )(fresh, cotangent, vectors, scale, turned, *(a for pair in saved for a in pair))
    return split_refs(found, [2] * 4 + [1] * 2)


def split_columns(shard, width):
    rows, columns = shard.shape
    return [shard[:, i : i + width] for i in range(0, columns, width)]


class Slice:
    def __init__(self, micro):
        self.micro, self.half = micro, micro // 2
        self.bits = self.half.bit_length() - 1
        self.chain, self.items = lax.axis_size("seg"), lax.axis_size("item")
        self.start = (self.chain - 2 * micro) // 2
        self.place, self.item = lax.axis_index("seg"), lax.axis_index("item")
        self.core = self.place % 2
        self.home = jnp.clip((self.place - self.start) // 2, 0, micro - 1)
        self.high, self.low = self.home // self.half, self.home % self.half
        self.at_home = jnp.logical_and(
            self.place >= self.start, self.place < self.start + 2 * micro
        )

    def seat(self, home, core=0):
        return self.start + 2 * home + core

    def far(self, home, core=0):
        return self.seat(home, core) + self.micro * (-1 if home < self.half else 1)

    def send(self, value, pairs):
        flat = [(a * self.items + x, b * self.items + x) for a, b in pairs for x in range(self.items)]
        return lax.ppermute(value, ("seg", "item"), flat)

    def send_across(self, value, bit):
        flat = []
        for i in range(self.micro):
            for c in range(2):
                at = self.seat(i, c) * self.items
                flat += [(at + x, at + (x ^ (1 << bit))) for x in range(self.items)]
        return lax.ppermute(value, ("seg", "item"), flat)

    def between_homes(self, flip):
        return [(self.seat(i, c), self.seat(i ^ flip, c)) for i in range(self.micro) for c in range(2)]

    def in_order(self, mine, got, side, axis):
        return jnp.where(
            side == 0, jnp.stack([mine, got], axis), jnp.stack([got, mine], axis)
        )

    def joined(self, mine, got, side, axis):
        return jnp.where(
            side == 0, jnp.concatenate([mine, got], axis), jnp.concatenate([got, mine], axis)
        )

    def gather(self, value, items=False):
        homes = [(i, c) for i in range(self.micro) for c in range(2)]
        got = self.send(value, [(self.far(i, c), self.seat(i, c)) for i, c in homes])
        whole = self.in_order(value, got, 1 - self.high, 0)
        if items:
            whole = whole.reshape((2,) + (2,) * (1 + self.bits) + value.shape[1:])
        whole = whole.reshape((1,) * (1 + self.bits) + whole.shape)
        for bit in range(self.bits + 1):
            axis = self.bits - bit
            side = (self.home >> bit) % 2
            out = whole
            if items:
                at = 2 + self.bits + axis
                out = lax.dynamic_index_in_dim(whole, 1 - side, at, keepdims=True)
                whole = lax.dynamic_index_in_dim(whole, side, at, keepdims=True)
            whole = self.joined(whole, self.send(out, self.between_homes(1 << bit)), side, axis)
        rest = value.shape[1:] if items else value.shape
        whole = whole.reshape((2, self.half, 2) + rest).swapaxes(1, 2)
        got = self.send(whole, [(self.seat(i, c), self.seat(i, 1 - c)) for i, c in homes])
        return self.in_order(whole, got, self.core, 3).reshape((self.chain,) + rest)

    def spread(self, values):
        kind = (2, 2, self.half, 2)
        parts = []
        for value in values:
            mine = value.reshape(kind + value.shape[1:])
            mine = lax.dynamic_index_in_dim(mine, self.core, 3, keepdims=False).swapaxes(1, 2)
            parts.append(mine.reshape((2,) * (1 + self.bits) + (2,) + value.shape[1:]))

        def cut(array, side, axis):
            return lax.dynamic_index_in_dim(array, side, axis, keepdims=False)

        wait = yield
        out = jnp.concatenate([cut(p, 1 - self.high + wait, 0) for p in parts], -2)
        got = self.send(out, self.between_homes(self.half))
        wait = yield after(out)
        own = jnp.concatenate([cut(p, self.high, 0) for p in parts], -2)

        def both(k):
            return jnp.stack([cut(p, k, self.bits) for p in (own, got)])

        homes = [(i, c) for i in range(self.micro) for c in range(2)]
        out = both(self.high + wait)
        got_away = self.send(out, [(self.seat(i, c), self.far(i, c)) for i, c in homes])
        wait = yield after(out)
        held = jnp.where(self.at_home, both(1 - self.high), got_away)
        near = (self.place // (2 * self.micro)) * self.half + (self.place // 2) % self.half
        flips = [0, self.half]
        for bit in reversed(range(self.bits)):
            side = (near >> bit) % 2
            out = cut(held, 1 - side + wait, 1)
            pairs = [
                (at(i, c), at(i ^ (1 << bit), c)) for i, c in homes for at in (self.seat, self.far)
            ]
            held = jnp.concatenate([cut(held, side, 1), self.send(out, pairs)])
            flips += [f ^ (1 << bit) for f in flips]
        yield after(out)
        order = jnp.array([flips.index(f) for f in range(self.micro)], jnp.int32)
        held = jnp.stack([cut(held, order[i ^ near], 0) for i in range(self.micro)])
        found, row = [], 0
        for value in values:
            found.append(held[:, row : row + value.shape[1]])
            row += value.shape[1]
        yield found

    def everywhere(self, value, wait):
        value = jnp.where(wait == 0, value, 0.0).astype(LOW)
        for stage in self.halvings("lhx"):
            value = add([value, self.exchange(value, stage)])
        homes = [(i, c) for i in range(self.micro) for c in range(2)]
        got = self.send(value, [(self.seat(i, c), self.far(i, c)) for i, c in homes])
        return jnp.where(self.at_home, value, got)

    def halvings(self, order):
        stages = []
        for name in order:
            if name == "x":
                stages += [("x", b) for b in range(self.items.bit_length() - 1)]
            elif name == "h":
                stages.append(("h", self.bits))
            else:
                stages += [("l", b) for b in range(self.bits)]
        return stages

    def side_of(self, stage):
        name, bit = stage
        return ((self.item if name == "x" else self.home) >> bit) % 2

    def exchange(self, out, stage):
        name, bit = stage
        if name == "x":
            return self.send_across(out, bit)
        return self.send(out, self.between_homes(1 << bit))

    def cut(self, term, stage, side):
        name, bit = stage
        axis = {"x": -1, "h": 0, "l": 1 + self.bits - bit}[name]
        found = []
        for f in term:
            size = f.shape[axis] // 2
            found.append(lax.dynamic_slice_in_dim(f, side * size, size, axis))
        return beside(found)

    def product(self, left, right):
        left, right = (jnp.where(self.core == 0, *pair) for pair in (left, right))
        left, right = (a.reshape(-1, a.shape[-1]) for a in (left, right))
        full = dot(left, right, TN).astype(LOW)
        kind = (2, 2) + (2,) * self.bits + (2,)
        return full.reshape(kind + (full.shape[0] // self.chain, full.shape[1]))

    def deliver(self, total):
        near = lax.dynamic_index_in_dim(total, 1 - self.high, 0, keepdims=False)
        away = lax.dynamic_index_in_dim(total, self.high, 0, keepdims=False)

        def of(pair, core):
            return lax.dynamic_index_in_dim(pair, core, 0, keepdims=False)

        homes = [(i, c) for i in range(self.micro) for c in range(2)]
        level = self.send(
            of(near, 1 - self.core), [(self.seat(i, c), self.seat(i, 1 - c)) for i, c in homes]
        )
        straight = self.send(
            of(away, self.core), [(self.seat(i, c), self.far(i, c)) for i, c in homes]
        )
        crossed = self.send(
            of(away, 1 - self.core), [(self.seat(i, c), self.far(i, 1 - c)) for i, c in homes]
        )
        same = jnp.where(self.at_home, of(near, self.core), straight)
        both = self.in_order(same, level + crossed, self.core, 0)
        if self.items == 2:
            swapped = lax.ppermute(both, "item", [(0, 1), (1, 0)])
            return [
                jnp.where(self.item == 0, both, swapped),
                jnp.where(self.item == 0, swapped, both),
            ]
        every = lax.all_gather(both, "item")
        width = self.items.bit_length() - 1
        return [every[int(format(x, "0%db" % width)[::-1], 2)] for x in range(self.items)]

    def reduce(self, chunks, values):
        stages = [self.halvings(order) for _, order in chunks]
        terms = [[[self.product(*p) for p in products]] for products, _ in chunks]
        wait = 0
        spread = self.spread(values)
        next(spread)
        for turn in range(len(stages[0])):
            outs = []
            for i, stage in enumerate(each[turn] for each in stages):
                side = self.side_of(stage)
                out = add([self.cut(f, stage, 1 - side + wait) for f in terms[i]])
                terms[i] = [[self.cut(f, stage, side)] for f in terms[i]]
                terms[i].append([self.exchange(out, stage)])
                outs.append(out)
            if turn < 3:
                shift = spread.send(wait)
            wait = after(outs[-1])
        wait = wait + shift
        values = spread.send(wait)
        sizes = [
            [(p[0][0].shape[-1] // self.chain, p[1][0].shape[-1]) for p in products]
            for products, _ in chunks
        ]
        rows = min(size[0] for each in sizes for size in each)
        totals = []
        for t in terms:
            total = add([f[0] for f in t])
            total = total.reshape((2, 2) + total.shape[-2:])
            strips = [total[:, :, i : i + rows] for i in range(0, total.shape[2], rows)]
            totals.append(strips[0] if len(strips) == 1 else jnp.concatenate(strips, -1))
        found = []
        for group in (range(len(totals)),):
            sides = self.deliver(jnp.concatenate([totals[i] for i in group], -1))
            at = 0
            for i in group:
                for high, wide in sizes[i]:
                    size = wide // self.items
                    strips = []
                    for _ in range(high // rows):
                        strips.append(
                            jnp.concatenate([side[..., at : at + size] for side in sides], -1)
                        )
                        at += size
                    found.append(jnp.concatenate(strips, 1).astype(F32))
        return found, values, wait


def beside(arrays):
    if len(arrays) == 1:
        return arrays[0]
    return jnp.concatenate(arrays, -1 if arrays[0].shape[-2] == arrays[-1].shape[-2] else -2)


def add(terms):
    total = terms[0].astype(F32)
    for t in terms[1:]:
        total = total + t.astype(F32)
    return total.astype(LOW)


def after(value):
    first, last = value[(0,) * value.ndim], value[(-1,) * value.ndim]
    return (first != first).astype(jnp.int32) + (last != last).astype(jnp.int32)


def body(text, cotangent, unroll, memory, *weights):
    micro, _, texts, width = text.shape
    mem = memory.shape[0]
    chain = lax.axis_size("seg")
    part = width // chain
    layers = (weights[:12], weights[12:])
    net = Slice(micro)

    def order(block):
        zero = jnp.zeros((block.shape[0], PAD - mem, width), block.dtype)
        return jnp.concatenate(
            [block[:, mem : mem + texts], block[:, :mem], zero, block[:, mem + texts :], zero], 1
        )

    def disorder(block):
        return jnp.concatenate(
            [
                block[:, texts : texts + mem],
                block[:, :texts],
                block[:, texts + PAD : texts + PAD + mem],
            ],
            1,
        )

    shards = []
    for w in layers:
        for matrix in (w[0], w[2], w[6], w[8]):
            shards += split_columns(matrix, width)
    gathered = lax.all_gather(jnp.concatenate(shards), "seg")
    if part % 16:
        gathered = regroup(gathered, 16 // (part & -part), part)
    text_home = net.gather(text[:, 0], items=True)
    cotangent_home = order(net.gather(cotangent[:, 0], items=True))
    vectors = jnp.concatenate([v for w in layers for v in w if v.ndim == 1])
    vectors = net.gather(vectors.reshape(-1, 2 * BLOCKS * part // 8)).reshape(chain, -1)
    vectors = vectors.astype(F32)
    rows_of = []
    at = 0
    for w in layers:
        for v in w:
            if v.ndim == 1:
                rows_of.append(vectors[:, at : at + v.shape[0]].reshape(-1, width))
                at += v.shape[0]
    half = len(rows_of) // 2
    table = jnp.stack([jnp.concatenate(rows_of[:half]), jnp.concatenate(rows_of[half:])])
    table = jnp.pad(table, ((0, 0), (0, 16 - table.shape[1]), (0, 0)))

    limit = unroll[net.home]
    segments = jnp.arange(chain, dtype=jnp.int32)
    fresh = jnp.logical_or(segments == 0, segments == limit).astype(jnp.int32)
    memory_rows = jnp.pad(memory, ((0, PAD - mem), (0, 0)))

    (low, qkv, probs, context, unit1, hidden, active, slope, unit2, (scale,), (out,), (turned,)) = (
        forward_chain(fresh, text_home, memory_rows, table, gathered)
    )
    (grad_qkv, grad_proj, grad_upper, grad_down, (text_grad,), (sums,)) = (
        backward_chain(
            fresh, cotangent_home, table, scale,
            (qkv, probs, unit1, slope, unit2), turned,
        )
    )

    (down, proj, up, qkv), (text_grad, layer_out), wait = net.reduce(
        [
            ([(active, grad_down), (context, grad_proj)], "lhx"),
            ([(hidden, grad_upper)], "hxl"),
            ([(low, grad_qkv)], "xlh"),
        ],
        [text_grad, out],
    )
    text_grad, layer_out = text_grad.astype(F32), disorder(layer_out)
    sums = net.everywhere(sums, wait).astype(F32)

    def own(row, rows):
        size = part * rows
        at = net.place * size
        return lax.dynamic_slice(sums, (row + at // width, at % width), (1, size)).reshape(-1)

    results = []
    for layer in range(2):
        base = 8 * layer
        vectors = [(base + 6, 2), (base + 5, 1), (base + 3, 1), (base + 4, 1)]
        vectors += [(16 + 4 * layer, 4), (base + 2, 1), (base, 1), (base + 1, 1)]
        left = [qkv[layer], proj[layer], up[layer], down[layer]]
        for w in layers[layer]:
            results.append(own(*vectors.pop(0)) if w.ndim == 1 else left.pop(0))
    memory_grad = lax.dynamic_slice(sums, (24, net.place * part), (mem, part))
    return (layer_out[:, None], text_grad[:, None], memory_grad, *results)


def regroup(gathered, together, part):
    shards, total, width = gathered.shape
    blocks = gathered.reshape(shards // together, together, total // part, part, width)
    pieces = []
    for layer in range(2):
        base = layer * BLOCKS
        for block in range(8):
            pieces.append(blocks[:, :, base + block])
        pieces.append(blocks[:, :, base + 8 : base + 12])
    return jnp.concatenate([p.reshape(shards // together, -1, width) for p in pieces], 1)


def solution(mesh):
    seg = (P("seg", None), P("seg"), P("seg", None)) + (P("seg"),) * 3
    seg = seg + (P("seg", None), P("seg"), P("seg", None)) + (P("seg"),) * 3
    rows = P("item", "seg", None, None)
    return jax.shard_map(
        body,
        mesh=mesh,
        in_specs=(rows, rows, P("item"), P()) + seg + seg,
        out_specs=(rows, rows, P(None, "seg")) + seg + seg,
        check_vma=False,
    )
```

```python
import functools

import jax
import jax.numpy as jnp
from jax import lax
from jax.experimental import pallas as pl
from jax.experimental.pallas import tpu as pltpu
from jax.sharding import PartitionSpec as P

HEAD_DIM = 64
EPSILON = 1e-05
F32 = jnp.float32
LOW = jnp.bfloat16
NN = (((1,), (0,)), ((), ()))
NT = (((1,), (1,)), ((), ()))
TN = (((0,), (0,)), ((), ()))

PAD = 16
BLOCKS = 12
B_QUERY, B_VALUE, B_OUT, GAIN1, SHIFT1, B_UP, B_DOWN, GAIN2, SHIFT2 = 0, 1, 2, 3, 4, 5, 9, 10, 11


def dot(left, right, dims=NN):
    return lax.dot_general(left, right, dims, preferred_element_type=F32)


def norm_rows(total, gain, shift):
    centre = total - jnp.mean(total, -1, keepdims=True)
    scale = lax.rsqrt(jnp.mean(centre * centre, -1, keepdims=True) + EPSILON)
    unit = centre * scale
    return unit, scale, unit * gain + shift


def norm_back(grad, unit, scale, gain):
    t = grad * gain
    return scale * (
        t - jnp.mean(t, -1, keepdims=True) - unit * jnp.mean(t * unit, -1, keepdims=True)
    )


def gelu_and_slope(upper):
    density = jnp.exp(upper * upper * -0.5) * 0.3989422804014327
    below = 0.5 * (1.0 + lax.erf(upper * 0.7071067811865476))
    return upper * below, below + upper * density


def fold(block):
    rows, width = block.shape
    return jnp.sum(block.reshape(rows // 8, 8, width), 0)


def two_heads(block, first):
    zero = jnp.zeros_like(block)
    return jnp.concatenate([jnp.where(first, block, zero), jnp.where(first, zero, block)], 0)


def copy_block(gathered, target, layer, block, part, sem):
    shards = gathered.shape[0]
    base = layer * BLOCKS * part

    def copy(shard, row, to, count):
        pltpu.make_async_copy(
            gathered.at[shard, pl.ds(pl.multiple_of(row, 16), count)],
            target(pl.multiple_of(to, 16), count),
            sem,
        ).start()

    @pl.when(block < 8)
    def _():
        def start(shard, none):
            copy(shard, base + block * part, shard * part, part)
            return none

        lax.fori_loop(0, shards, start, 0)

    @pl.when(block >= 8)
    def _():
        def start(i, none):
            shard = (block - 8) * (shards // 4) + i
            copy(shard, base + 8 * part, i * 4 * part, 4 * part)
            return none

        lax.fori_loop(0, shards // 4, start, 0)


def block_of(held, index, width):
    return held.at[pl.ds(pl.multiple_of(index * width, 128), width), :]


def start_weights(gathered, held, width, sems):
    part = width // gathered.shape[0]

    def start(index, none):
        def target(row, count):
            return held.at[pl.ds(pl.multiple_of(index * width + row, 16), count)]

        copy_block(gathered, target, index // BLOCKS, index % BLOCKS, part, sems.at[index])
        return none

    lax.fori_loop(0, 2 * BLOCKS, start, 0)


def start_turned(turned, held, width, sems):
    lanes = width // 128
    per = lanes + lanes // 2
    for index in reversed(range(2 * BLOCKS)):
        for lane in range(lanes):
            block, k = divmod(index * lanes + lane, per)
            for rows, at, part in parts_of(k, width):
                pltpu.make_async_copy(
                    turned.at[block, rows, at : at + 128],
                    held.at[
                        index * width + part.start : index * width + part.stop,
                        128 * lane : 128 * (lane + 1),
                    ],
                    sems.at[index],
                ).start()


def wait_block(held, index, width, sems):
    target = block_of(held, index, width)
    pltpu.make_async_copy(target, target, sems.at[index]).wait()


def split_refs(refs, sizes):
    parts = []
    for size in sizes:
        parts.append(refs[:size])
        refs = refs[size:]
    return parts


def forward_kernel(*refs):
    (
        (fresh_ref, text_ref, memory_ref, vector_ref, gathered_ref),
        low_ref, qkv_ref, probs_ref, context_ref, unit1_ref, hidden_ref, active_ref, slope_ref,
        unit2_ref,
        (scale_ref, out_ref, turned_ref, held, carry, sems),
    ) = split_refs(refs, [5] + [2] * 9 + [6])
    step = pl.program_id(0)
    texts, width = text_ref.shape[1:]
    rows = texts + 2 * PAD
    mem = 10
    first_head = lax.broadcasted_iota(jnp.int32, (rows, 2 * HEAD_DIM), 1) < HEAD_DIM

    def run():
        column = lax.broadcasted_iota(jnp.int32, (2 * rows, rows), 1)
        unused = jnp.logical_or(
            column >= texts + PAD + mem,
            jnp.logical_and(column >= texts + mem, column < texts + PAD),
        )
        mask = jnp.where(unused, -1e30, 0.0).astype(F32)
        memory = memory_ref[...]
        read = jnp.where(fresh_ref[step] > 0, memory, carry[...])
        x = jnp.concatenate([text_ref[0], read, memory], 0).astype(F32)
        scales = []
        for index in range(2):

            def weight(block, index=index):
                at = index * BLOCKS + block
                return held[at * width : (at + 1) * width, :]

            def vector(row, index=index):
                return vector_ref[index, row : row + 1, :]

            low = x.astype(LOW)
            low_ref[index][0] = low
            query = (dot(low, weight(0)) + vector(B_QUERY)).astype(LOW)
            keys = dot(low, weight(1)).astype(LOW)
            values = (dot(low, weight(2)) + vector(B_VALUE)).astype(LOW)
            qkv_ref[index][0, :, :width] = query
            qkv_ref[index][0, :, width : 2 * width] = keys
            qkv_ref[index][0, :, 2 * width :] = values
            query = query * LOW(HEAD_DIM ** (-0.5))
            pairs = range(width // (2 * HEAD_DIM))
            cols = [slice(2 * HEAD_DIM * p, 2 * HEAD_DIM * (p + 1)) for p in pairs]
            scores = [dot(two_heads(query[:, c], first_head), keys[:, c], NT) + mask for c in cols]
            weights = [jnp.exp(e - jnp.max(e, -1, keepdims=True)) for e in scores]
            totals = [jnp.sum(e, -1, keepdims=True) for e in weights]
            both = [dot(weights[p].astype(LOW), values[:, cols[p]]) for p in pairs]
            for p in pairs:
                inverse = 1.0 / totals[p]
                context = both[p] * inverse
                probs_ref[index][0, p] = (weights[p] * inverse).astype(LOW)
                context_ref[index][0, :, cols[p]] = jnp.where(
                    first_head, context[:rows], context[rows:]
                ).astype(LOW)
            total = x + dot(context_ref[index][0], weight(3)) + vector(B_OUT)
            unit, scale, hidden = norm_rows(total, vector(GAIN1), vector(SHIFT1))
            unit1_ref[index][0] = unit.astype(LOW)
            scales.append(scale)
            hidden_low = hidden.astype(LOW)
            hidden_ref[index][0] = hidden_low
            total = hidden + vector(B_DOWN)
            ahead = dot(hidden_low, weight(4)) + vector(B_UP)
            for block in range(4):
                wide = slice(block * width, (block + 1) * width)
                upper = ahead
                if block < 3:
                    ahead = dot(hidden_low, weight(5 + block)) + vector(B_UP + block + 1)
                active, slope = gelu_and_slope(upper)
                active = active.astype(LOW)
                active_ref[index][0, :, wide] = active
                slope_ref[index][0, :, wide] = slope.astype(LOW)
                total = total + dot(active, weight(8 + block))
            unit, scale, x = norm_rows(total, vector(GAIN2), vector(SHIFT2))
            unit2_ref[index][0] = unit.astype(LOW)
            scales.append(scale)
        lane = lax.broadcasted_iota(jnp.int32, (rows, 128), 1)
        packed = scales[3]
        for i in (2, 1, 0):
            packed = jnp.where(lane < 32 * (i + 1), scales[i], packed)
        scale_ref[0] = packed
        final = x.astype(LOW)
        out_ref[0] = final
        carry[...] = final[texts + PAD :]

    @pl.when(step == 0)
    def _():
        start_weights(gathered_ref, held, width, sems)
        for block in range(2 * BLOCKS):
            wait_block(held, block, width, sems)
        carry[...] = jnp.zeros_like(carry)

    run()

    steps = turns_of(pl.num_programs(0))
    lanes = width // 128
    per = lanes + lanes // 2

    def turn(k):
        row = pl.multiple_of(((step // steps) * per + k) * 128, 128)
        strip = held[pl.ds(row, 128), :].T
        for rows, at, part in parts_of(k, width):
            turned_ref[0, rows, at : at + 128] = strip[part]

    for k in range(per):
        if steps == 1:
            turn(k)
        else:
            pl.when(step % steps == k % steps)(functools.partial(turn, k))


def parts_of(k, width):
    lanes = width // 128
    if k < lanes:
        return [(slice(0, width), 128 * k, slice(0, width))]
    half, at = width // 2, 256 * (k - lanes)
    return [
        (slice(width, width + half), at + 128 * i, slice(half * i, half * (i + 1))) for i in range(2)
    ]


def turns_of(segments):
    return max(segments // 16, 1)


def backward_kernel(*refs):
    (
        (fresh_ref, cotangent_ref, vector_ref, scale_ref, turned_ref),
        qkv_ref, probs_ref, unit1_ref, slope_ref, unit2_ref,
        grad_qkv_ref, grad_proj_ref, grad_upper_ref, grad_down_ref,
        (text_ref, table_ref, narrow_ref, wide_ref, memory_ref, held, carry, sems),
    ) = split_refs(refs, [5] + [2] * 5 + [2] * 4 + [8])
    turn = pl.program_id(0)
    step = pl.num_programs(0) - 1 - turn
    rows, width = cotangent_ref.shape[1:]
    texts = rows - 2 * PAD
    first_head = lax.broadcasted_iota(jnp.int32, (rows, 2 * HEAD_DIM), 1) < HEAD_DIM

    def run(loading):
        grad = cotangent_ref[0].astype(F32)
        if not loading:
            grad = jnp.concatenate(
                [grad[: texts + PAD], grad[texts + PAD :] + carry[...].astype(F32)], 0
            )
        for index in (1, 0):

            def weight(block, index=index):
                at = index * BLOCKS + block
                if loading:
                    wait_block(held, at, width, sems)
                return held[at * width : (at + 1) * width, :]

            def vector(row, index=index):
                return vector_ref[index, row : row + 1, :]

            def scale(norm, index=index):
                lane = 32 * (2 * index + norm)
                return scale_ref[0, :, lane : lane + 1]

            unit = unit2_ref[index][0].astype(F32)
            narrow_ref[index, 0] += fold(grad * unit)
            narrow_ref[index, 1] += fold(grad)
            grad_second = norm_back(grad, unit, scale(1), vector(GAIN2))
            narrow_ref[index, 2] += fold(grad_second)
            grad_down = grad_second.astype(LOW)
            grad_hidden = grad_second
            ahead = dot(grad_down, weight(11))
            for block in (3, 2, 1, 0):
                wide = slice(block * width, (block + 1) * width)
                grad_upper = ahead * slope_ref[index][0, :, wide].astype(F32)
                if block:
                    ahead = dot(grad_down, weight(7 + block))
                wide_ref[index, block] += fold(grad_upper)
                grad_upper = grad_upper.astype(LOW)
                grad_upper_ref[index][0, :, wide] = grad_upper
                grad_hidden = grad_hidden + dot(grad_upper, weight(4 + block))
            grad_down_ref[index][0] = grad_down
            unit = unit1_ref[index][0].astype(F32)
            narrow_ref[index, 3] += fold(grad_hidden * unit)
            narrow_ref[index, 4] += fold(grad_hidden)
            grad_first = norm_back(grad_hidden, unit, scale(0), vector(GAIN1))
            narrow_ref[index, 5] += fold(grad_first)
            grad_proj = grad_first.astype(LOW)
            grad_proj_ref[index][0] = grad_proj
            grad_context = dot(grad_proj, weight(3)).astype(LOW)
            eighth = LOW(HEAD_DIM ** (-0.5))
            pairs = range(width // (2 * HEAD_DIM))
            cols = [slice(2 * HEAD_DIM * p, 2 * HEAD_DIM * (p + 1)) for p in pairs]
            in_keys = [slice(width + c.start, width + c.stop) for c in cols]
            in_values = [slice(2 * width + c.start, 2 * width + c.stop) for c in cols]
            query = [two_heads(qkv_ref[index][0, :, c] * eighth, first_head) for c in cols]
            context = [two_heads(grad_context[:, c], first_head) for c in cols]
            term = [dot(context[p], qkv_ref[index][0, :, in_values[p]], NT) for p in pairs]
            probs = [probs_ref[index][0, p] for p in pairs]
            grad_values = [dot(probs[p], context[p], TN) for p in pairs]
            for p in pairs:
                narrow_ref[index, 7, :, cols[p]] += fold(grad_values[p])
                grad_qkv_ref[index][0, :, in_values[p]] = grad_values[p].astype(LOW)
            by_values = dot(grad_qkv_ref[index][0, :, 2 * width :], weight(2))
            term = [term[p] * probs[p].astype(F32) for p in pairs]
            total = [jnp.sum(t, -1, keepdims=True) for t in term]
            grad_scores = [(term[p] - probs[p].astype(F32) * total[p]).astype(LOW) for p in pairs]
            both = [dot(grad_scores[p], qkv_ref[index][0, :, in_keys[p]] * eighth) for p in pairs]
            grad_query = [jnp.where(first_head, b[:rows], b[rows:]) for b in both]
            grad_keys = [dot(grad_scores[p], query[p], TN) for p in pairs]
            for p in pairs:
                narrow_ref[index, 6, :, cols[p]] += fold(grad_query[p])
                grad_qkv_ref[index][0, :, cols[p]] = grad_query[p].astype(LOW)
                grad_qkv_ref[index][0, :, in_keys[p]] = grad_keys[p].astype(LOW)
            grad = grad_first + by_values
            for block in (1, 0):
                cols = slice(block * width, (block + 1) * width)
                grad = grad + dot(grad_qkv_ref[index][0, :, cols], weight(block))
        text_ref[0] = grad[:texts].astype(LOW)
        read = grad[texts : texts + PAD]
        fresh = fresh_ref[step] > 0
        memory_ref[...] += grad[texts + PAD :] + jnp.where(fresh, read, 0.0)
        carry[...] = jnp.where(fresh, 0.0, read).astype(LOW)

    @pl.when(turn == 0)
    def _():
        start_turned(turned_ref, held, width, sems)
        narrow_ref[...] = jnp.zeros_like(narrow_ref)
        wide_ref[...] = jnp.zeros_like(wide_ref)
        memory_ref[...] = jnp.zeros_like(memory_ref)
        run(True)

    @pl.when(turn > 0)
    def _():
        run(False)

    @pl.when(step == 0)
    def _():
        sums = [jnp.sum(narrow_ref[i, j], 0, keepdims=True) for i in range(2) for j in range(8)]
        sums += [jnp.sum(wide_ref[i, j], 0, keepdims=True) for i in range(2) for j in range(4)]
        table_ref[...] = jnp.concatenate(sums + [memory_ref[...]], 0)


SMEM = pl.BlockSpec(memory_space=pltpu.SMEM)
VMEM = pl.BlockSpec(memory_space=pltpu.VMEM)
ANY = pl.BlockSpec(memory_space=pl.ANY)


def cost(rows, width, segments):
    return pl.CostEstimate(
        flops=2 * rows * 2 * BLOCKS * width * width * segments * 4,
        bytes_accessed=2 * 2 * BLOCKS * width * width,
        transcendentals=0,
    )


def forward_chain(fresh, text, memory, vectors, gathered):
    segments, texts, width = text.shape
    rows = texts + 2 * PAD
    pairs = width // (2 * HEAD_DIM)

    def block(shape):
        return pl.BlockSpec((1,) + shape, lambda s: (s,) + (0,) * len(shape))

    row = (rows, width)
    shapes = [row, (rows, 3 * width), (pairs, 2 * rows, rows), row, row, row]
    shapes += [(rows, 4 * width), (rows, 4 * width), row]
    outs = [(shape, LOW) for shape in shapes for _ in range(2)]
    outs += [((rows, 128), F32), (row, LOW)]
    steps = turns_of(segments)
    found = pl.pallas_call(
        forward_kernel,
        grid=(segments,),
        in_specs=[SMEM, block((texts, width)), VMEM, VMEM, ANY],
        out_specs=[block(shape) for shape, _ in outs]
        + [pl.BlockSpec((1,) + gathered.shape[1:], lambda s: (s // steps, 0, 0))],
        out_shape=[jax.ShapeDtypeStruct((segments,) + shape, kind) for shape, kind in outs]
        + [jax.ShapeDtypeStruct(gathered.shape, LOW)],
        input_output_aliases={4: len(outs)} if steps > 1 else {},
        scratch_shapes=[
            pltpu.VMEM((2 * BLOCKS * width, width), LOW),
            pltpu.VMEM((PAD, width), LOW),
            pltpu.SemaphoreType.DMA((2 * BLOCKS,)),
        ],
        compiler_params=pltpu.CompilerParams(vmem_limit_bytes=62 << 20),
        cost_estimate=cost(rows, width, segments),
        name="forward_chain",
    )(fresh, text, memory, vectors, gathered)
    return split_refs(found, [2] * 9 + [1, 1, 1])


def backward_chain(fresh, cotangent, vectors, scale, saved, turned):
    segments, rows, width = cotangent.shape
    texts = rows - 2 * PAD
    pairs = width // (2 * HEAD_DIM)

    def block(shape):
        return pl.BlockSpec((1,) + shape, lambda t: (segments - 1 - t,) + (0,) * len(shape))

    row, three, four = (rows, width), (rows, 3 * width), (rows, 4 * width)
    outs = [shape for shape in (three, row, four, row) for _ in range(2)] + [(texts, width)]
    ins = [shape for shape in (three, (pairs, 2 * rows, rows), row, four, row) for _ in range(2)]
    found = pl.pallas_call(
        backward_kernel,
        grid=(segments,),
        in_specs=[SMEM, block(row), VMEM, block((rows, 128)), ANY]
        + [block(shape) for shape in ins],
        out_specs=[block(shape) for shape in outs] + [VMEM],
        out_shape=[jax.ShapeDtypeStruct((segments,) + shape, LOW) for shape in outs]
        + [jax.ShapeDtypeStruct((24 + PAD, width), F32)],
        scratch_shapes=[
            pltpu.VMEM((2, 8, 8, width), F32),
            pltpu.VMEM((2, 4, 8, width), F32),
            pltpu.VMEM((PAD, width), F32),
            pltpu.VMEM((2 * BLOCKS * width, width), LOW),
            pltpu.VMEM((PAD, width), LOW),
            pltpu.SemaphoreType.DMA((2 * BLOCKS,)),
        ],
        input_output_aliases={5: 0, 6: 1, 9: 2, 10: 3, 11: 4, 12: 5, 13: 6, 14: 7},
        compiler_params=pltpu.CompilerParams(vmem_limit_bytes=62 << 20),
        cost_estimate=cost(rows, width, segments),
        name="backward_chain",
    )(fresh, cotangent, vectors, scale, turned, *(a for pair in saved for a in pair))
    return split_refs(found, [2] * 4 + [1] * 2)


def pack_kernel(*refs):
    *shards, out_ref = refs
    width = out_ref.shape[1]
    row = 0
    for ref in shards:
        rows, columns = ref.shape
        for at in range(0, columns, width):
            out_ref[row : row + rows] = ref[:, at : at + width]
            row += rows


def pack(matrices, width):
    rows = sum(m.size for m in matrices) // width
    return pl.pallas_call(
        pack_kernel,
        in_specs=[VMEM] * len(matrices),
        out_specs=VMEM,
        out_shape=jax.ShapeDtypeStruct((rows, width), LOW),
        name="pack",
    )(*matrices)


def split_columns(shard, width):
    rows, columns = shard.shape
    return [shard[:, i : i + width] for i in range(0, columns, width)]


class Slice:
    def __init__(self, micro):
        self.micro, self.half = micro, micro // 2
        self.bits = self.half.bit_length() - 1
        self.chain, self.items = lax.axis_size("seg"), lax.axis_size("item")
        self.start = (self.chain - 2 * micro) // 2
        self.place, self.item = lax.axis_index("seg"), lax.axis_index("item")
        self.core = self.place % 2
        self.home = jnp.clip((self.place - self.start) // 2, 0, micro - 1)
        self.high, self.low = self.home // self.half, self.home % self.half
        self.at_home = jnp.logical_and(
            self.place >= self.start, self.place < self.start + 2 * micro
        )

    def seat(self, home, core=0):
        return self.start + 2 * home + core

    def far(self, home, core=0):
        return self.seat(home, core) + self.micro * (-1 if home < self.half else 1)

    def send(self, value, pairs):
        flat = [(a * self.items + x, b * self.items + x) for a, b in pairs for x in range(self.items)]
        return lax.ppermute(value, ("seg", "item"), flat)

    def send_across(self, value, bit):
        flat = []
        for i in range(self.micro):
            for c in range(2):
                at = self.seat(i, c) * self.items
                flat += [(at + x, at + (x ^ (1 << bit))) for x in range(self.items)]
        return lax.ppermute(value, ("seg", "item"), flat)

    def between_homes(self, flip):
        return [(self.seat(i, c), self.seat(i ^ flip, c)) for i in range(self.micro) for c in range(2)]

    def in_order(self, mine, got, side, axis):
        return jnp.where(
            side == 0, jnp.stack([mine, got], axis), jnp.stack([got, mine], axis)
        )

    def joined(self, mine, got, side, axis):
        return jnp.where(
            side == 0, jnp.concatenate([mine, got], axis), jnp.concatenate([got, mine], axis)
        )

    def gather(self, value, items=False):
        homes = [(i, c) for i in range(self.micro) for c in range(2)]
        got = self.send(value, [(self.far(i, c), self.seat(i, c)) for i, c in homes])
        whole = self.in_order(value, got, 1 - self.high, 0)
        if items:
            whole = whole.reshape((2,) + (2,) * (1 + self.bits) + value.shape[1:])
        whole = whole.reshape((1,) * (1 + self.bits) + whole.shape)
        for bit in range(self.bits + 1):
            axis = self.bits - bit
            side = (self.home >> bit) % 2
            out = whole
            if items:
                at = 2 + self.bits + axis
                out = lax.dynamic_index_in_dim(whole, 1 - side, at, keepdims=True)
                whole = lax.dynamic_index_in_dim(whole, side, at, keepdims=True)
            whole = self.joined(whole, self.send(out, self.between_homes(1 << bit)), side, axis)
        rest = value.shape[1:] if items else value.shape
        whole = whole.reshape((2, self.half, 2) + rest).swapaxes(1, 2)
        got = self.send(whole, [(self.seat(i, c), self.seat(i, 1 - c)) for i, c in homes])
        return self.in_order(whole, got, self.core, 3).reshape((self.chain,) + rest)

    def spread(self, values):
        kind = (2, 2, self.half, 2)
        parts = []
        for value in values:
            mine = value.reshape(kind + value.shape[1:])
            mine = lax.dynamic_index_in_dim(mine, self.core, 3, keepdims=False).swapaxes(1, 2)
            parts.append(mine.reshape((2,) * (1 + self.bits) + (2,) + value.shape[1:]))

        def cut(array, side, axis):
            return lax.dynamic_index_in_dim(array, side, axis, keepdims=False)

        wait = yield
        out = jnp.concatenate([cut(p, 1 - self.high + wait, 0) for p in parts], -2)
        got = self.send(out, self.between_homes(self.half))
        wait = yield after(out)
        own = jnp.concatenate([cut(p, self.high, 0) for p in parts], -2)

        def both(k):
            return jnp.stack([cut(p, k, self.bits) for p in (own, got)])

        homes = [(i, c) for i in range(self.micro) for c in range(2)]
        out = both(self.high + wait)
        got_away = self.send(out, [(self.seat(i, c), self.far(i, c)) for i, c in homes])
        wait = yield after(out)
        held = jnp.where(self.at_home, both(1 - self.high), got_away)
        near = (self.place // (2 * self.micro)) * self.half + (self.place // 2) % self.half
        flips = [0, self.half]
        for bit in reversed(range(self.bits)):
            side = (near >> bit) % 2
            out = cut(held, 1 - side + wait, 1)
            pairs = [
                (at(i, c), at(i ^ (1 << bit), c)) for i, c in homes for at in (self.seat, self.far)
            ]
            held = jnp.concatenate([cut(held, side, 1), self.send(out, pairs)])
            flips += [f ^ (1 << bit) for f in flips]
        yield after(out)
        order = jnp.array([flips.index(f) for f in range(self.micro)], jnp.int32)
        held = jnp.stack([cut(held, order[i ^ near], 0) for i in range(self.micro)])
        found, row = [], 0
        for value in values:
            found.append(held[:, row : row + value.shape[1]])
            row += value.shape[1]
        yield found

    def everywhere(self, value, wait):
        value = jnp.where(wait == 0, value, 0.0).astype(LOW)
        for stage in self.halvings("lhx"):
            value = add([value, self.exchange(value, stage)])
        homes = [(i, c) for i in range(self.micro) for c in range(2)]
        got = self.send(value, [(self.seat(i, c), self.far(i, c)) for i, c in homes])
        return jnp.where(self.at_home, value, got)

    def halvings(self, order):
        stages = []
        for name in order:
            if name == "x":
                stages += [("x", b) for b in range(self.items.bit_length() - 1)]
            elif name == "h":
                stages.append(("h", self.bits))
            else:
                stages += [("l", b) for b in range(self.bits)]
        return stages

    def side_of(self, stage):
        name, bit = stage
        return ((self.item if name == "x" else self.home) >> bit) % 2

    def exchange(self, out, stage):
        name, bit = stage
        if name == "x":
            return self.send_across(out, bit)
        return self.send(out, self.between_homes(1 << bit))

    def cut(self, term, stage, side):
        name, bit = stage
        axis = {"x": -1, "h": 0, "l": 1 + self.bits - bit}[name]
        found = []
        for f in term:
            size = f.shape[axis] // 2
            found.append(lax.dynamic_slice_in_dim(f, side * size, size, axis))
        return beside(found)

    def product(self, left, right):
        left, right = (jnp.where(self.core == 0, *pair) for pair in (left, right))
        left, right = (a.reshape(-1, a.shape[-1]) for a in (left, right))
        full = dot(left, right, TN).astype(LOW)
        kind = (2, 2) + (2,) * self.bits + (2,)
        return full.reshape(kind + (full.shape[0] // self.chain, full.shape[1]))

    def deliver(self, total):
        near = lax.dynamic_index_in_dim(total, 1 - self.high, 0, keepdims=False)
        away = lax.dynamic_index_in_dim(total, self.high, 0, keepdims=False)

        def of(pair, core):
            return lax.dynamic_index_in_dim(pair, core, 0, keepdims=False)

        homes = [(i, c) for i in range(self.micro) for c in range(2)]
        level = self.send(
            of(near, 1 - self.core), [(self.seat(i, c), self.seat(i, 1 - c)) for i, c in homes]
        )
        straight = self.send(
            of(away, self.core), [(self.seat(i, c), self.far(i, c)) for i, c in homes]
        )
        crossed = self.send(
            of(away, 1 - self.core), [(self.seat(i, c), self.far(i, 1 - c)) for i, c in homes]
        )
        same = jnp.where(self.at_home, of(near, self.core), straight)
        both = self.in_order(same, level + crossed, self.core, 0)
        if self.items == 2:
            swapped = lax.ppermute(both, "item", [(0, 1), (1, 0)])
            return [
                jnp.where(self.item == 0, both, swapped),
                jnp.where(self.item == 0, swapped, both),
            ]
        every = lax.all_gather(both, "item")
        width = self.items.bit_length() - 1
        return [every[int(format(x, "0%db" % width)[::-1], 2)] for x in range(self.items)]

    def reduce(self, chunks, values):
        stages = [self.halvings(order) for _, order in chunks]
        terms = [[[self.product(*p) for p in products]] for products, _ in chunks]
        wait = 0
        spread = self.spread(values)
        next(spread)
        for turn in range(len(stages[0])):
            outs = []
            for i, stage in enumerate(each[turn] for each in stages):
                side = self.side_of(stage)
                out = add([self.cut(f, stage, 1 - side + wait) for f in terms[i]])
                terms[i] = [[self.cut(f, stage, side)] for f in terms[i]]
                terms[i].append([self.exchange(out, stage)])
                outs.append(out)
            if turn < 3:
                shift = spread.send(wait)
            wait = after(outs[-1])
        wait = wait + shift
        values = spread.send(wait)
        sizes = [
            [(p[0][0].shape[-1] // self.chain, p[1][0].shape[-1]) for p in products]
            for products, _ in chunks
        ]
        rows = min(size[0] for each in sizes for size in each)
        totals = []
        for t in terms:
            total = add([f[0] for f in t])
            total = total.reshape((2, 2) + total.shape[-2:])
            strips = [total[:, :, i : i + rows] for i in range(0, total.shape[2], rows)]
            totals.append(strips[0] if len(strips) == 1 else jnp.concatenate(strips, -1))
        found = []
        for group in (range(len(totals)),):
            sides = self.deliver(jnp.concatenate([totals[i] for i in group], -1))
            at = 0
            for i in group:
                for high, wide in sizes[i]:
                    size = wide // self.items
                    strips = []
                    for _ in range(high // rows):
                        strips.append(
                            jnp.concatenate([side[..., at : at + size] for side in sides], -1)
                        )
                        at += size
                    found.append(jnp.concatenate(strips, 1).astype(F32))
        return found, values, wait


def beside(arrays):
    if len(arrays) == 1:
        return arrays[0]
    return jnp.concatenate(arrays, -1 if arrays[0].shape[-2] == arrays[-1].shape[-2] else -2)


def add(terms):
    total = terms[0].astype(F32)
    for t in terms[1:]:
        total = total + t.astype(F32)
    return total.astype(LOW)


def after(value):
    first, last = value[(0,) * value.ndim], value[(-1,) * value.ndim]
    return (first != first).astype(jnp.int32) + (last != last).astype(jnp.int32)


def body(text, cotangent, unroll, memory, *weights):
    micro, _, texts, width = text.shape
    mem = memory.shape[0]
    chain = lax.axis_size("seg")
    part = width // chain
    layers = (weights[:12], weights[12:])
    net = Slice(micro)

    def order(block):
        zero = jnp.zeros((block.shape[0], PAD - mem, width), block.dtype)
        return jnp.concatenate(
            [block[:, mem : mem + texts], block[:, :mem], zero, block[:, mem + texts :], zero], 1
        )

    def disorder(block):
        return jnp.concatenate(
            [
                block[:, texts : texts + mem],
                block[:, :texts],
                block[:, texts + PAD : texts + PAD + mem],
            ],
            1,
        )

    matrices = [m for w in layers for m in (w[0], w[2], w[6], w[8])]
    if part % 16:
        shard = jnp.concatenate([c for m in matrices for c in split_columns(m, width)])
    else:
        shard = pack(matrices, width)
    gathered = lax.all_gather(shard, "seg")
    if part % 16:
        gathered = regroup(gathered, 16 // (part & -part), part)
    text_home = net.gather(text[:, 0], items=True)
    cotangent_home = order(net.gather(cotangent[:, 0], items=True))
    vectors = jnp.concatenate([v for w in layers for v in w if v.ndim == 1])
    vectors = net.gather(vectors.reshape(-1, 2 * BLOCKS * part // 8)).reshape(chain, -1)
    vectors = vectors.astype(F32)
    rows_of = []
    at = 0
    for w in layers:
        for v in w:
            if v.ndim == 1:
                rows_of.append(vectors[:, at : at + v.shape[0]].reshape(-1, width))
                at += v.shape[0]
    half = len(rows_of) // 2
    table = jnp.stack([jnp.concatenate(rows_of[:half]), jnp.concatenate(rows_of[half:])])
    table = jnp.pad(table, ((0, 0), (0, 16 - table.shape[1]), (0, 0)))

    limit = unroll[net.home]
    segments = jnp.arange(chain, dtype=jnp.int32)
    fresh = jnp.logical_or(segments == 0, segments == limit).astype(jnp.int32)
    memory_rows = jnp.pad(memory, ((0, PAD - mem), (0, 0)))

    (low, qkv, probs, context, unit1, hidden, active, slope, unit2, (scale,), (out,), (turned,)) = (
        forward_chain(fresh, text_home, memory_rows, table, gathered)
    )
    (grad_qkv, grad_proj, grad_upper, grad_down, (text_grad,), (sums,)) = (
        backward_chain(
            fresh, cotangent_home, table, scale,
            (qkv, probs, unit1, slope, unit2), turned,
        )
    )

    (down, up, qkv, proj), (text_grad, layer_out), wait = net.reduce(
        [
            ([(active, grad_down)], "lhx"),
            ([(hidden, grad_upper)], "hxl"),
            ([(low, grad_qkv), (context, grad_proj)], "xlh"),
        ],
        [text_grad, out],
    )
    text_grad, layer_out = text_grad.astype(F32), disorder(layer_out)
    sums = net.everywhere(sums, wait).astype(F32)

    def own(row, rows):
        size = part * rows
        at = net.place * size
        return lax.dynamic_slice(sums, (row + at // width, at % width), (1, size)).reshape(-1)

    results = []
    for layer in range(2):
        base = 8 * layer
        vectors = [(base + 6, 2), (base + 5, 1), (base + 3, 1), (base + 4, 1)]
        vectors += [(16 + 4 * layer, 4), (base + 2, 1), (base, 1), (base + 1, 1)]
        left = [qkv[layer], proj[layer], up[layer], down[layer]]
        for w in layers[layer]:
            results.append(own(*vectors.pop(0)) if w.ndim == 1 else left.pop(0))
    memory_grad = lax.dynamic_slice(sums, (24, net.place * part), (mem, part))
    return (layer_out[:, None], text_grad[:, None], memory_grad, *results)


def regroup(gathered, together, part):
    shards, total, width = gathered.shape
    blocks = gathered.reshape(shards // together, together, total // part, part, width)
    pieces = []
    for layer in range(2):
        base = layer * BLOCKS
        for block in range(8):
            pieces.append(blocks[:, :, base + block])
        pieces.append(blocks[:, :, base + 8 : base + 12])
    return jnp.concatenate([p.reshape(shards // together, -1, width) for p in pieces], 1)


def solution(mesh):
    seg = (P("seg", None), P("seg"), P("seg", None)) + (P("seg"),) * 3
    seg = seg + (P("seg", None), P("seg"), P("seg", None)) + (P("seg"),) * 3
    rows = P("item", "seg", None, None)
    return jax.shard_map(
        body,
        mesh=mesh,
        in_specs=(rows, rows, P("item"), P()) + seg + seg,
        out_specs=(rows, rows, P(None, "seg")) + seg + seg,
        check_vma=False,
    )
```

```python
import functools

import jax
import jax.numpy as jnp
from jax import lax
from jax.experimental import pallas as pl
from jax.experimental.pallas import tpu as pltpu
from jax.sharding import PartitionSpec as P

HEAD_DIM = 64
EPSILON = 1e-05
F32 = jnp.float32
LOW = jnp.bfloat16
NN = (((1,), (0,)), ((), ()))
NT = (((1,), (1,)), ((), ()))
TN = (((0,), (0,)), ((), ()))

PAD = 16
BLOCKS = 12
B_QUERY, B_VALUE, B_OUT, GAIN1, SHIFT1, B_UP, B_DOWN, GAIN2, SHIFT2 = 0, 1, 2, 3, 4, 5, 9, 10, 11


def dot(left, right, dims=NN):
    return lax.dot_general(left, right, dims, preferred_element_type=F32)


def norm_rows(total, gain, shift):
    centre = total - jnp.mean(total, -1, keepdims=True)
    scale = lax.rsqrt(jnp.mean(centre * centre, -1, keepdims=True) + EPSILON)
    unit = centre * scale
    return unit, scale, unit * gain + shift


def norm_back(grad, unit, scale, gain):
    t = grad * gain
    return scale * (
        t - jnp.mean(t, -1, keepdims=True) - unit * jnp.mean(t * unit, -1, keepdims=True)
    )


def gelu_and_slope(upper):
    density = jnp.exp(upper * upper * -0.5) * 0.3989422804014327
    below = 0.5 * (1.0 + lax.erf(upper * 0.7071067811865476))
    return upper * below, below + upper * density


def fold(block):
    rows, width = block.shape
    return jnp.sum(block.reshape(rows // 8, 8, width), 0)


def two_heads(block, first):
    zero = jnp.zeros_like(block)
    return jnp.concatenate([jnp.where(first, block, zero), jnp.where(first, zero, block)], 0)


def copy_block(gathered, target, layer, block, part, sem):
    shards = gathered.shape[0]
    base = layer * BLOCKS * part

    def copy(shard, row, to, count):
        pltpu.make_async_copy(
            gathered.at[shard, pl.ds(pl.multiple_of(row, 16), count)],
            target(pl.multiple_of(to, 16), count),
            sem,
        ).start()

    @pl.when(block < 8)
    def _():
        def start(shard, none):
            copy(shard, base + block * part, shard * part, part)
            return none

        lax.fori_loop(0, shards, start, 0)

    @pl.when(block >= 8)
    def _():
        def start(i, none):
            shard = (block - 8) * (shards // 4) + i
            copy(shard, base + 8 * part, i * 4 * part, 4 * part)
            return none

        lax.fori_loop(0, shards // 4, start, 0)


def block_of(held, index, width):
    return held.at[pl.ds(pl.multiple_of(index * width, 128), width), :]


def start_weights(gathered, held, width, sems):
    part = width // gathered.shape[0]

    def start(index, none):
        def target(row, count):
            return held.at[pl.ds(pl.multiple_of(index * width + row, 16), count)]

        copy_block(gathered, target, index // BLOCKS, index % BLOCKS, part, sems.at[index])
        return none

    lax.fori_loop(0, 2 * BLOCKS, start, 0)


def start_turned(turned, held, width, sems):
    lanes = width // 128
    per = lanes + lanes // 2
    for index in reversed(range(2 * BLOCKS)):
        for lane in range(lanes):
            block, k = divmod(index * lanes + lane, per)
            for rows, at, part in parts_of(k, width):
                pltpu.make_async_copy(
                    turned.at[block, rows, at : at + 128],
                    held.at[
                        index * width + part.start : index * width + part.stop,
                        128 * lane : 128 * (lane + 1),
                    ],
                    sems.at[index],
                ).start()


def wait_block(held, index, width, sems):
    target = block_of(held, index, width)
    pltpu.make_async_copy(target, target, sems.at[index]).wait()


def split_refs(refs, sizes):
    parts = []
    for size in sizes:
        parts.append(refs[:size])
        refs = refs[size:]
    return parts


def forward_kernel(*refs):
    (
        (fresh_ref, text_ref, memory_ref, vector_ref, gathered_ref),
        low_ref, qkv_ref, probs_ref, context_ref, unit1_ref, hidden_ref, active_ref, slope_ref,
        unit2_ref,
        (scale_ref, out_ref, turned_ref, held, carry, sems),
    ) = split_refs(refs, [5] + [2] * 9 + [6])
    step = pl.program_id(0)
    texts, width = text_ref.shape[1:]
    rows = texts + 2 * PAD
    mem = 10
    first_head = lax.broadcasted_iota(jnp.int32, (rows, 2 * HEAD_DIM), 1) < HEAD_DIM

    def run():
        column = lax.broadcasted_iota(jnp.int32, (2 * rows, rows), 1)
        unused = jnp.logical_or(
            column >= texts + PAD + mem,
            jnp.logical_and(column >= texts + mem, column < texts + PAD),
        )
        mask = jnp.where(unused, -1e30, 0.0).astype(F32)
        memory = memory_ref[...]
        read = jnp.where(fresh_ref[step] > 0, memory, carry[...])
        x = jnp.concatenate([text_ref[0], read, memory], 0).astype(F32)
        scales = []
        for index in range(2):

            def weight(block, index=index):
                at = index * BLOCKS + block
                return held[at * width : (at + 1) * width, :]

            def vector(row, index=index):
                return vector_ref[index, row : row + 1, :]

            low = x.astype(LOW)
            low_ref[index][0] = low
            query = (dot(low, weight(0)) + vector(B_QUERY)).astype(LOW)
            keys = dot(low, weight(1)).astype(LOW)
            values = (dot(low, weight(2)) + vector(B_VALUE)).astype(LOW)
            qkv_ref[index][0, :, :width] = query
            qkv_ref[index][0, :, width : 2 * width] = keys
            qkv_ref[index][0, :, 2 * width :] = values
            query = query * LOW(HEAD_DIM ** (-0.5))
            pairs = range(width // (2 * HEAD_DIM))
            cols = [slice(2 * HEAD_DIM * p, 2 * HEAD_DIM * (p + 1)) for p in pairs]
            scores = [dot(two_heads(query[:, c], first_head), keys[:, c], NT) + mask for c in cols]
            weights = [jnp.exp(e - jnp.max(e, -1, keepdims=True)) for e in scores]
            totals = [jnp.sum(e, -1, keepdims=True) for e in weights]
            both = [dot(weights[p].astype(LOW), values[:, cols[p]]) for p in pairs]
            for p in pairs:
                inverse = 1.0 / totals[p]
                context = both[p] * inverse
                probs_ref[index][0, p] = (weights[p] * inverse).astype(LOW)
                context_ref[index][0, :, cols[p]] = jnp.where(
                    first_head, context[:rows], context[rows:]
                ).astype(LOW)
            total = x + vector(B_OUT)
            for part in range(0, width, 256):
                total = total + dot(
                    context_ref[index][0, :, part : part + 256], weight(3)[part : part + 256]
                )
            unit, scale, hidden = norm_rows(total, vector(GAIN1), vector(SHIFT1))
            unit1_ref[index][0] = unit.astype(LOW)
            scales.append(scale)
            hidden_low = hidden.astype(LOW)
            hidden_ref[index][0] = hidden_low
            total = hidden + vector(B_DOWN)
            ahead = dot(hidden_low, weight(4)) + vector(B_UP)
            for block in range(4):
                wide = slice(block * width, (block + 1) * width)
                upper = ahead
                if block < 3:
                    ahead = dot(hidden_low, weight(5 + block)) + vector(B_UP + block + 1)
                active, slope = gelu_and_slope(upper)
                active = active.astype(LOW)
                active_ref[index][0, :, wide] = active
                slope_ref[index][0, :, wide] = slope.astype(LOW)
                total = total + dot(active, weight(8 + block))
            unit, scale, x = norm_rows(total, vector(GAIN2), vector(SHIFT2))
            unit2_ref[index][0] = unit.astype(LOW)
            scales.append(scale)
        lane = lax.broadcasted_iota(jnp.int32, (rows, 128), 1)
        packed = scales[3]
        for i in (2, 1, 0):
            packed = jnp.where(lane < 32 * (i + 1), scales[i], packed)
        scale_ref[0] = packed
        final = x.astype(LOW)
        out_ref[0] = final
        carry[...] = final[texts + PAD :]

    @pl.when(step == 0)
    def _():
        start_weights(gathered_ref, held, width, sems)
        for block in range(2 * BLOCKS):
            wait_block(held, block, width, sems)
        carry[...] = jnp.zeros_like(carry)

    run()

    steps = turns_of(pl.num_programs(0))
    lanes = width // 128
    per = lanes + lanes // 2

    def turn(k):
        row = pl.multiple_of(((step // steps) * per + k) * 128, 128)
        strip = held[pl.ds(row, 128), :].T
        for rows, at, part in parts_of(k, width):
            turned_ref[0, rows, at : at + 128] = strip[part]

    for k in range(per):
        if steps == 1:
            turn(k)
        else:
            pl.when(step % steps == k % steps)(functools.partial(turn, k))


def parts_of(k, width):
    lanes = width // 128
    if k < lanes:
        return [(slice(0, width), 128 * k, slice(0, width))]
    half, at = width // 2, 256 * (k - lanes)
    return [
        (slice(width, width + half), at + 128 * i, slice(half * i, half * (i + 1))) for i in range(2)
    ]


def turns_of(segments):
    return max(segments // 16, 1)


def backward_kernel(*refs):
    (
        (fresh_ref, cotangent_ref, vector_ref, scale_ref, turned_ref),
        qkv_ref, probs_ref, unit1_ref, slope_ref, unit2_ref,
        grad_qkv_ref, grad_proj_ref, grad_upper_ref, grad_down_ref,
        (text_ref, table_ref, narrow_ref, wide_ref, memory_ref, held, carry, sems),
    ) = split_refs(refs, [5] + [2] * 5 + [2] * 4 + [8])
    turn = pl.program_id(0)
    step = pl.num_programs(0) - 1 - turn
    rows, width = cotangent_ref.shape[1:]
    texts = rows - 2 * PAD
    first_head = lax.broadcasted_iota(jnp.int32, (rows, 2 * HEAD_DIM), 1) < HEAD_DIM

    def run(loading):
        grad = cotangent_ref[0].astype(F32)
        if not loading:
            grad = jnp.concatenate(
                [grad[: texts + PAD], grad[texts + PAD :] + carry[...].astype(F32)], 0
            )
        for index in (1, 0):

            def weight(block, index=index):
                at = index * BLOCKS + block
                if loading:
                    wait_block(held, at, width, sems)
                return held[at * width : (at + 1) * width, :]

            def vector(row, index=index):
                return vector_ref[index, row : row + 1, :]

            def scale(norm, index=index):
                lane = 32 * (2 * index + norm)
                return scale_ref[0, :, lane : lane + 1]

            unit = unit2_ref[index][0].astype(F32)
            narrow_ref[index, 0] += fold(grad * unit)
            narrow_ref[index, 1] += fold(grad)
            grad_second = norm_back(grad, unit, scale(1), vector(GAIN2))
            narrow_ref[index, 2] += fold(grad_second)
            grad_down = grad_second.astype(LOW)
            grad_hidden = grad_second
            ahead = dot(grad_down, weight(11))
            for block in (3, 2, 1, 0):
                wide = slice(block * width, (block + 1) * width)
                grad_upper = ahead * slope_ref[index][0, :, wide].astype(F32)
                if block:
                    ahead = dot(grad_down, weight(7 + block))
                wide_ref[index, block] += fold(grad_upper)
                grad_upper = grad_upper.astype(LOW)
                grad_upper_ref[index][0, :, wide] = grad_upper
                grad_hidden = grad_hidden + dot(grad_upper, weight(4 + block))
            grad_down_ref[index][0] = grad_down
            unit = unit1_ref[index][0].astype(F32)
            narrow_ref[index, 3] += fold(grad_hidden * unit)
            narrow_ref[index, 4] += fold(grad_hidden)
            grad_first = norm_back(grad_hidden, unit, scale(0), vector(GAIN1))
            narrow_ref[index, 5] += fold(grad_first)
            grad_proj = grad_first.astype(LOW)
            grad_proj_ref[index][0] = grad_proj
            grad_context = dot(grad_proj, weight(3)).astype(LOW)
            eighth = LOW(HEAD_DIM ** (-0.5))
            pairs = range(width // (2 * HEAD_DIM))
            cols = [slice(2 * HEAD_DIM * p, 2 * HEAD_DIM * (p + 1)) for p in pairs]
            in_keys = [slice(width + c.start, width + c.stop) for c in cols]
            in_values = [slice(2 * width + c.start, 2 * width + c.stop) for c in cols]
            query = [two_heads(qkv_ref[index][0, :, c] * eighth, first_head) for c in cols]
            context = [two_heads(grad_context[:, c], first_head) for c in cols]
            term = [dot(context[p], qkv_ref[index][0, :, in_values[p]], NT) for p in pairs]
            probs = [probs_ref[index][0, p] for p in pairs]
            grad_values = [dot(probs[p], context[p], TN) for p in pairs]
            for p in pairs:
                narrow_ref[index, 7, :, cols[p]] += fold(grad_values[p])
                grad_qkv_ref[index][0, :, in_values[p]] = grad_values[p].astype(LOW)
            by_values = dot(grad_qkv_ref[index][0, :, 2 * width :], weight(2))
            term = [term[p] * probs[p].astype(F32) for p in pairs]
            total = [jnp.sum(t, -1, keepdims=True) for t in term]
            grad_scores = [(term[p] - probs[p].astype(F32) * total[p]).astype(LOW) for p in pairs]
            both = [dot(grad_scores[p], qkv_ref[index][0, :, in_keys[p]] * eighth) for p in pairs]
            grad_query = [jnp.where(first_head, b[:rows], b[rows:]) for b in both]
            grad_keys = [dot(grad_scores[p], query[p], TN) for p in pairs]
            for p in pairs:
                narrow_ref[index, 6, :, cols[p]] += fold(grad_query[p])
                grad_qkv_ref[index][0, :, cols[p]] = grad_query[p].astype(LOW)
                grad_qkv_ref[index][0, :, in_keys[p]] = grad_keys[p].astype(LOW)
            grad = grad_first + by_values
            for block in (1, 0):
                cols = slice(block * width, (block + 1) * width)
                grad = grad + dot(grad_qkv_ref[index][0, :, cols], weight(block))
        text_ref[0] = grad[:texts].astype(LOW)
        read = grad[texts : texts + PAD]
        fresh = fresh_ref[step] > 0
        memory_ref[...] += grad[texts + PAD :] + jnp.where(fresh, read, 0.0)
        carry[...] = jnp.where(fresh, 0.0, read).astype(LOW)

    @pl.when(turn == 0)
    def _():
        start_turned(turned_ref, held, width, sems)
        narrow_ref[...] = jnp.zeros_like(narrow_ref)
        wide_ref[...] = jnp.zeros_like(wide_ref)
        memory_ref[...] = jnp.zeros_like(memory_ref)
        run(True)

    @pl.when(turn > 0)
    def _():
        run(False)

    @pl.when(step == 0)
    def _():
        sums = [jnp.sum(narrow_ref[i, j], 0, keepdims=True) for i in range(2) for j in range(8)]
        sums += [jnp.sum(wide_ref[i, j], 0, keepdims=True) for i in range(2) for j in range(4)]
        table_ref[...] = jnp.concatenate(sums + [memory_ref[...]], 0)


SMEM = pl.BlockSpec(memory_space=pltpu.SMEM)
VMEM = pl.BlockSpec(memory_space=pltpu.VMEM)
ANY = pl.BlockSpec(memory_space=pl.ANY)


def cost(rows, width, segments):
    return pl.CostEstimate(
        flops=2 * rows * 2 * BLOCKS * width * width * segments * 4,
        bytes_accessed=2 * 2 * BLOCKS * width * width,
        transcendentals=0,
    )


def forward_chain(fresh, text, memory, vectors, gathered):
    segments, texts, width = text.shape
    rows = texts + 2 * PAD
    pairs = width // (2 * HEAD_DIM)

    def block(shape):
        return pl.BlockSpec((1,) + shape, lambda s: (s,) + (0,) * len(shape))

    row = (rows, width)
    shapes = [row, (rows, 3 * width), (pairs, 2 * rows, rows), row, row, row]
    shapes += [(rows, 4 * width), (rows, 4 * width), row]
    outs = [(shape, LOW) for shape in shapes for _ in range(2)]
    outs += [((rows, 128), F32), (row, LOW)]
    steps = turns_of(segments)
    found = pl.pallas_call(
        forward_kernel,
        grid=(segments,),
        in_specs=[SMEM, block((texts, width)), VMEM, VMEM, ANY],
        out_specs=[block(shape) for shape, _ in outs]
        + [pl.BlockSpec((1,) + gathered.shape[1:], lambda s: (s // steps, 0, 0))],
        out_shape=[jax.ShapeDtypeStruct((segments,) + shape, kind) for shape, kind in outs]
        + [jax.ShapeDtypeStruct(gathered.shape, LOW)],
        input_output_aliases={4: len(outs)} if steps > 1 else {},
        scratch_shapes=[
            pltpu.VMEM((2 * BLOCKS * width, width), LOW),
            pltpu.VMEM((PAD, width), LOW),
            pltpu.SemaphoreType.DMA((2 * BLOCKS,)),
        ],
        compiler_params=pltpu.CompilerParams(vmem_limit_bytes=62 << 20),
        cost_estimate=cost(rows, width, segments),
        name="forward_chain",
    )(fresh, text, memory, vectors, gathered)
    return split_refs(found, [2] * 9 + [1, 1, 1])


def backward_chain(fresh, cotangent, vectors, scale, saved, turned):
    segments, rows, width = cotangent.shape
    texts = rows - 2 * PAD
    pairs = width // (2 * HEAD_DIM)

    def block(shape):
        return pl.BlockSpec((1,) + shape, lambda t: (segments - 1 - t,) + (0,) * len(shape))

    row, three, four = (rows, width), (rows, 3 * width), (rows, 4 * width)
    outs = [shape for shape in (three, row, four, row) for _ in range(2)] + [(texts, width)]
    ins = [shape for shape in (three, (pairs, 2 * rows, rows), row, four, row) for _ in range(2)]
    found = pl.pallas_call(
        backward_kernel,
        grid=(segments,),
        in_specs=[SMEM, block(row), VMEM, block((rows, 128)), ANY]
        + [block(shape) for shape in ins],
        out_specs=[block(shape) for shape in outs] + [VMEM],
        out_shape=[jax.ShapeDtypeStruct((segments,) + shape, LOW) for shape in outs]
        + [jax.ShapeDtypeStruct((24 + PAD, width), F32)],
        scratch_shapes=[
            pltpu.VMEM((2, 8, 8, width), F32),
            pltpu.VMEM((2, 4, 8, width), F32),
            pltpu.VMEM((PAD, width), F32),
            pltpu.VMEM((2 * BLOCKS * width, width), LOW),
            pltpu.VMEM((PAD, width), LOW),
            pltpu.SemaphoreType.DMA((2 * BLOCKS,)),
        ],
        input_output_aliases={5: 0, 6: 1, 9: 2, 10: 3, 11: 4, 12: 5, 13: 6, 14: 7},
        compiler_params=pltpu.CompilerParams(vmem_limit_bytes=62 << 20),
        cost_estimate=cost(rows, width, segments),
        name="backward_chain",
    )(fresh, cotangent, vectors, scale, turned, *(a for pair in saved for a in pair))
    return split_refs(found, [2] * 4 + [1] * 2)


def pack_kernel(*refs):
    *shards, out_ref = refs
    width = out_ref.shape[1]
    row = 0
    for ref in shards:
        rows, columns = ref.shape
        for at in range(0, columns, width):
            out_ref[row : row + rows] = ref[:, at : at + width]
            row += rows


def pack(matrices, width):
    rows = sum(m.size for m in matrices) // width
    return pl.pallas_call(
        pack_kernel,
        in_specs=[VMEM] * len(matrices),
        out_specs=VMEM,
        out_shape=jax.ShapeDtypeStruct((rows, width), LOW),
        name="pack",
    )(*matrices)


def split_columns(shard, width):
    rows, columns = shard.shape
    return [shard[:, i : i + width] for i in range(0, columns, width)]


class Slice:
    def __init__(self, micro):
        self.micro, self.half = micro, micro // 2
        self.bits = self.half.bit_length() - 1
        self.chain, self.items = lax.axis_size("seg"), lax.axis_size("item")
        self.start = (self.chain - 2 * micro) // 2
        self.place, self.item = lax.axis_index("seg"), lax.axis_index("item")
        self.core = self.place % 2
        self.home = jnp.clip((self.place - self.start) // 2, 0, micro - 1)
        self.high, self.low = self.home // self.half, self.home % self.half
        self.at_home = jnp.logical_and(
            self.place >= self.start, self.place < self.start + 2 * micro
        )

    def seat(self, home, core=0):
        return self.start + 2 * home + core

    def far(self, home, core=0):
        return self.seat(home, core) + self.micro * (-1 if home < self.half else 1)

    def send(self, value, pairs):
        flat = [(a * self.items + x, b * self.items + x) for a, b in pairs for x in range(self.items)]
        return lax.ppermute(value, ("seg", "item"), flat)

    def send_across(self, value, bit):
        flat = []
        for i in range(self.micro):
            for c in range(2):
                at = self.seat(i, c) * self.items
                flat += [(at + x, at + (x ^ (1 << bit))) for x in range(self.items)]
        return lax.ppermute(value, ("seg", "item"), flat)

    def between_homes(self, flip):
        return [(self.seat(i, c), self.seat(i ^ flip, c)) for i in range(self.micro) for c in range(2)]

    def in_order(self, mine, got, side, axis):
        return jnp.where(
            side == 0, jnp.stack([mine, got], axis), jnp.stack([got, mine], axis)
        )

    def joined(self, mine, got, side, axis):
        return jnp.where(
            side == 0, jnp.concatenate([mine, got], axis), jnp.concatenate([got, mine], axis)
        )

    def gather(self, value, items=False):
        homes = [(i, c) for i in range(self.micro) for c in range(2)]
        got = self.send(value, [(self.far(i, c), self.seat(i, c)) for i, c in homes])
        whole = self.in_order(value, got, 1 - self.high, 0)
        if items:
            whole = whole.reshape((2,) + (2,) * (1 + self.bits) + value.shape[1:])
        whole = whole.reshape((1,) * (1 + self.bits) + whole.shape)
        for bit in range(self.bits + 1):
            axis = self.bits - bit
            side = (self.home >> bit) % 2
            out = whole
            if items:
                at = 2 + self.bits + axis
                out = lax.dynamic_index_in_dim(whole, 1 - side, at, keepdims=True)
                whole = lax.dynamic_index_in_dim(whole, side, at, keepdims=True)
            whole = self.joined(whole, self.send(out, self.between_homes(1 << bit)), side, axis)
        rest = value.shape[1:] if items else value.shape
        whole = whole.reshape((2, self.half, 2) + rest).swapaxes(1, 2)
        got = self.send(whole, [(self.seat(i, c), self.seat(i, 1 - c)) for i, c in homes])
        return self.in_order(whole, got, self.core, 3).reshape((self.chain,) + rest)

    def spread(self, values):
        kind = (2, 2, self.half, 2)
        parts = []
        for value in values:
            mine = value.reshape(kind + value.shape[1:])
            mine = lax.dynamic_index_in_dim(mine, self.core, 3, keepdims=False).swapaxes(1, 2)
            parts.append(mine.reshape((2,) * (1 + self.bits) + (2,) + value.shape[1:]))

        def cut(array, side, axis):
            return lax.dynamic_index_in_dim(array, side, axis, keepdims=False)

        wait = yield
        out = jnp.concatenate([cut(p, 1 - self.high + wait, 0) for p in parts], -2)
        got = self.send(out, self.between_homes(self.half))
        wait = yield after(out)
        own = jnp.concatenate([cut(p, self.high, 0) for p in parts], -2)

        def both(k):
            return jnp.stack([cut(p, k, self.bits) for p in (own, got)])

        homes = [(i, c) for i in range(self.micro) for c in range(2)]
        out = both(self.high + wait)
        got_away = self.send(out, [(self.seat(i, c), self.far(i, c)) for i, c in homes])
        wait = yield after(out)
        held = jnp.where(self.at_home, both(1 - self.high), got_away)
        near = (self.place // (2 * self.micro)) * self.half + (self.place // 2) % self.half
        flips = [0, self.half]
        for bit in reversed(range(self.bits)):
            side = (near >> bit) % 2
            out = cut(held, 1 - side + wait, 1)
            pairs = [
                (at(i, c), at(i ^ (1 << bit), c)) for i, c in homes for at in (self.seat, self.far)
            ]
            held = jnp.concatenate([cut(held, side, 1), self.send(out, pairs)])
            flips += [f ^ (1 << bit) for f in flips]
        yield after(out)
        order = jnp.array([flips.index(f) for f in range(self.micro)], jnp.int32)
        held = jnp.stack([cut(held, order[i ^ near], 0) for i in range(self.micro)])
        found, row = [], 0
        for value in values:
            found.append(held[:, row : row + value.shape[1]])
            row += value.shape[1]
        yield found

    def everywhere(self, value, wait):
        value = jnp.where(wait == 0, value, 0.0).astype(LOW)
        for stage in self.halvings("lhx"):
            value = add([value, self.exchange(value, stage)])
        homes = [(i, c) for i in range(self.micro) for c in range(2)]
        got = self.send(value, [(self.seat(i, c), self.far(i, c)) for i, c in homes])
        return jnp.where(self.at_home, value, got)

    def halvings(self, order):
        stages = []
        for name in order:
            if name == "x":
                stages += [("x", b) for b in range(self.items.bit_length() - 1)]
            elif name == "h":
                stages.append(("h", self.bits))
            else:
                stages += [("l", b) for b in range(self.bits)]
        return stages

    def side_of(self, stage):
        name, bit = stage
        return ((self.item if name == "x" else self.home) >> bit) % 2

    def exchange(self, out, stage):
        name, bit = stage
        if name == "x":
            return self.send_across(out, bit)
        return self.send(out, self.between_homes(1 << bit))

    def cut(self, term, stage, side):
        name, bit = stage
        axis = {"x": -1, "h": 0, "l": 1 + self.bits - bit}[name]
        found = []
        for f in term:
            size = f.shape[axis] // 2
            found.append(lax.dynamic_slice_in_dim(f, side * size, size, axis))
        return beside(found)

    def product(self, left, right):
        left, right = (jnp.where(self.core == 0, *pair) for pair in (left, right))
        left, right = (a.reshape(-1, a.shape[-1]) for a in (left, right))
        full = dot(left, right, TN).astype(LOW)
        kind = (2, 2) + (2,) * self.bits + (2,)
        return full.reshape(kind + (full.shape[0] // self.chain, full.shape[1]))

    def deliver(self, total):
        near = lax.dynamic_index_in_dim(total, 1 - self.high, 0, keepdims=False)
        away = lax.dynamic_index_in_dim(total, self.high, 0, keepdims=False)

        def of(pair, core):
            return lax.dynamic_index_in_dim(pair, core, 0, keepdims=False)

        homes = [(i, c) for i in range(self.micro) for c in range(2)]
        level = self.send(
            of(near, 1 - self.core), [(self.seat(i, c), self.seat(i, 1 - c)) for i, c in homes]
        )
        straight = self.send(
            of(away, self.core), [(self.seat(i, c), self.far(i, c)) for i, c in homes]
        )
        crossed = self.send(
            of(away, 1 - self.core), [(self.seat(i, c), self.far(i, 1 - c)) for i, c in homes]
        )
        same = jnp.where(self.at_home, of(near, self.core), straight)
        both = self.in_order(same, level + crossed, self.core, 0)
        if self.items == 2:
            swapped = lax.ppermute(both, "item", [(0, 1), (1, 0)])
            return [
                jnp.where(self.item == 0, both, swapped),
                jnp.where(self.item == 0, swapped, both),
            ]
        every = lax.all_gather(both, "item")
        width = self.items.bit_length() - 1
        return [every[int(format(x, "0%db" % width)[::-1], 2)] for x in range(self.items)]

    def reduce(self, chunks, values):
        stages = [self.halvings(order) for _, order in chunks]
        terms = [[[self.product(*p) for p in products]] for products, _ in chunks]
        wait = 0
        spread = self.spread(values)
        next(spread)
        for turn in range(len(stages[0])):
            outs = []
            for i, stage in enumerate(each[turn] for each in stages):
                side = self.side_of(stage)
                out = add([self.cut(f, stage, 1 - side) for f in terms[i]])
                terms[i] = [[self.cut(f, stage, side)] for f in terms[i]]
                terms[i].append([self.exchange(out, stage)])
                outs.append(out)
            if turn < 3:
                shift = spread.send(wait)
            wait = after(outs[-1])
        wait = wait + shift
        values = spread.send(wait)
        sizes = [
            [(p[0][0].shape[-1] // self.chain, p[1][0].shape[-1]) for p in products]
            for products, _ in chunks
        ]
        rows = min(size[0] for each in sizes for size in each)
        totals = []
        for t in terms:
            total = add([f[0] for f in t])
            total = total.reshape((2, 2) + total.shape[-2:])
            strips = [total[:, :, i : i + rows] for i in range(0, total.shape[2], rows)]
            totals.append(strips[0] if len(strips) == 1 else jnp.concatenate(strips, -1))
        found = []
        for group in (range(len(totals)),):
            sides = self.deliver(jnp.concatenate([totals[i] for i in group], -1))
            at = 0
            for i in group:
                for high, wide in sizes[i]:
                    size = wide // self.items
                    strips = []
                    for _ in range(high // rows):
                        strips.append(
                            jnp.concatenate([side[..., at : at + size] for side in sides], -1)
                        )
                        at += size
                    found.append(jnp.concatenate(strips, 1).astype(F32))
        return found, values, wait


def beside(arrays):
    if len(arrays) == 1:
        return arrays[0]
    return jnp.concatenate(arrays, -1 if arrays[0].shape[-2] == arrays[-1].shape[-2] else -2)


def add(terms):
    total = terms[0].astype(F32)
    for t in terms[1:]:
        total = total + t.astype(F32)
    return total.astype(LOW)


def after(value):
    first, last = value[(0,) * value.ndim], value[(-1,) * value.ndim]
    return (first != first).astype(jnp.int32) + (last != last).astype(jnp.int32)


def body(text, cotangent, unroll, memory, *weights):
    micro, _, texts, width = text.shape
    mem = memory.shape[0]
    chain = lax.axis_size("seg")
    part = width // chain
    layers = (weights[:12], weights[12:])
    net = Slice(micro)

    def order(block):
        zero = jnp.zeros((block.shape[0], PAD - mem, width), block.dtype)
        return jnp.concatenate(
            [block[:, mem : mem + texts], block[:, :mem], zero, block[:, mem + texts :], zero], 1
        )

    def disorder(block):
        return jnp.concatenate(
            [
                block[:, texts : texts + mem],
                block[:, :texts],
                block[:, texts + PAD : texts + PAD + mem],
            ],
            1,
        )

    matrices = [m for w in layers for m in (w[0], w[2], w[6], w[8])]
    if part % 16:
        shard = jnp.concatenate([c for m in matrices for c in split_columns(m, width)])
    else:
        shard = pack(matrices, width)
    gathered = lax.all_gather(shard, "seg")
    if part % 16:
        gathered = regroup(gathered, 16 // (part & -part), part)
    text_home = net.gather(text[:, 0], items=True)
    if chain > 16:
        cotangent_home = order(net.gather(cotangent[:, 0], items=True))
    else:
        later = jnp.where(after(gathered) == 0, order(cotangent[:, 0]), 0)
        cotangent_home = lax.dynamic_index_in_dim(
            lax.all_gather(later, "seg"), net.home, 1, keepdims=False
        )
    vectors = jnp.concatenate([v for w in layers for v in w if v.ndim == 1])
    vectors = net.gather(vectors.reshape(-1, 2 * BLOCKS * part // 8)).reshape(chain, -1)
    vectors = vectors.astype(F32)
    rows_of = []
    at = 0
    for w in layers:
        for v in w:
            if v.ndim == 1:
                rows_of.append(vectors[:, at : at + v.shape[0]].reshape(-1, width))
                at += v.shape[0]
    half = len(rows_of) // 2
    table = jnp.stack([jnp.concatenate(rows_of[:half]), jnp.concatenate(rows_of[half:])])
    table = jnp.pad(table, ((0, 0), (0, 16 - table.shape[1]), (0, 0)))

    limit = unroll[net.home]
    segments = jnp.arange(chain, dtype=jnp.int32)
    fresh = jnp.logical_or(segments == 0, segments == limit).astype(jnp.int32)
    memory_rows = jnp.pad(memory, ((0, PAD - mem), (0, 0)))

    (low, qkv, probs, context, unit1, hidden, active, slope, unit2, (scale,), (out,), (turned,)) = (
        forward_chain(fresh, text_home, memory_rows, table, gathered)
    )
    (grad_qkv, grad_proj, grad_upper, grad_down, (text_grad,), (sums,)) = (
        backward_chain(
            fresh, cotangent_home, table, scale,
            (qkv, probs, unit1, slope, unit2), turned,
        )
    )

    (down, up, qkv, proj), (text_grad, layer_out), wait = net.reduce(
        [
            ([(active, grad_down)], "lhx"),
            ([(hidden, grad_upper)], "hxl"),
            ([(low, grad_qkv), (context, grad_proj)], "xlh"),
        ],
        [text_grad, out],
    )
    text_grad, layer_out = text_grad.astype(F32), disorder(layer_out)
    sums = net.everywhere(sums, wait).astype(F32)

    def own(row, rows):
        size = part * rows
        at = net.place * size
        return lax.dynamic_slice(sums, (row + at // width, at % width), (1, size)).reshape(-1)

    results = []
    for layer in range(2):
        base = 8 * layer
        vectors = [(base + 6, 2), (base + 5, 1), (base + 3, 1), (base + 4, 1)]
        vectors += [(16 + 4 * layer, 4), (base + 2, 1), (base, 1), (base + 1, 1)]
        left = [qkv[layer], proj[layer], up[layer], down[layer]]
        for w in layers[layer]:
            results.append(own(*vectors.pop(0)) if w.ndim == 1 else left.pop(0))
    memory_grad = lax.dynamic_slice(sums, (24, net.place * part), (mem, part))
    return (layer_out[:, None], text_grad[:, None], memory_grad, *results)


def regroup(gathered, together, part):
    shards, total, width = gathered.shape
    blocks = gathered.reshape(shards // together, together, total // part, part, width)
    pieces = []
    for layer in range(2):
        base = layer * BLOCKS
        for block in range(8):
            pieces.append(blocks[:, :, base + block])
        pieces.append(blocks[:, :, base + 8 : base + 12])
    return jnp.concatenate([p.reshape(shards // together, -1, width) for p in pieces], 1)


def solution(mesh):
    seg = (P("seg", None), P("seg"), P("seg", None)) + (P("seg"),) * 3
    seg = seg + (P("seg", None), P("seg"), P("seg", None)) + (P("seg"),) * 3
    rows = P("item", "seg", None, None)
    return jax.shard_map(
        body,
        mesh=mesh,
        in_specs=(rows, rows, P("item"), P()) + seg + seg,
        out_specs=(rows, rows, P(None, "seg")) + seg + seg,
        check_vma=False,
    )
```
